32 devices in a mesh: dp: 8 (over z, x), mp: 4 (over y, core).
Axes of the slice: x: 2, y: 2, z: 4, core: 2. Of those that a mesh axis runs over, the one named last changes fastest.
Arguments:
- layer_input: bfloat16 [4096, 4096], P('dp'), may hold values from -40 to 40
- gate_pre: bfloat16 [4096, 5120], P('dp', 'mp'), may hold values from -5 to 5
- up_pre: bfloat16 [4096, 5120], P('dp', 'mp'), may hold values from -5 to 5
- hidden_cot: bfloat16 [4096, 5120], P('dp', 'mp'), may hold values from -6 to 6
- teacher_ids: int32 [4096], P('dp'), may hold values from 0 to 63
- adv_table: float32 [64], replicated, may hold values from 0.25 to 2
- gate_weight: bfloat16 [4096, 5120], P('dp', 'mp'), may hold values from -0.09375 to 0.09375
- up_weight: bfloat16 [4096, 5120], P('dp', 'mp'), may hold values from -0.09375 to 0.09375
- row_moments: float32 [2, 4096], P(None, 'dp'), may hold values from 0.05 to 0.5
- col_moments: float32 [2, 5120], P(None, 'mp'), may hold values from 0.05 to 0.5
Outputs:
- input_grad: bfloat16 [4096, 4096], P('dp', 'mp')
- gate_update: float32 [4096, 5120], P('dp', 'mp')
- up_update: float32 [4096, 5120], P('dp', 'mp')
- new_rows: float32 [2, 4096], P(None, 'dp')
- new_cols: float32 [2, 5120], P(None, 'mp')
The draws below stay inside these ranges and needn't reach their ends.
All inputs are finite; a program needn't handle non-finite values.
Results may differ from the reference program's by a relative error of at most 0.011.
Values may be sent and summed in bfloat16 or wider, within the bound.
No kernel may reach another device: no remote copies, remote signals or barrier semaphores. Data moves between devices by JAX's collectives and lax.ppermute only.
A program may use at most 192 MiB of HBM per device.

```python
import math
import jax
import jax.numpy as jnp
from jax import lax

D = 4096
FF = 5120
TOK_DEV = 512
CLASSES = 64
TOKENS = 4096
N_DP = 8


def draw_layer_input(key, part):
    key = jax.random.fold_in(key, 11)
    key_base, key_cols, key_rows = jax.random.split(key, 3)
    ramp = 3.0 ** (jnp.arange(D, dtype=jnp.float32) / D)
    column_scale = ramp * jnp.exp(jax.random.uniform(key_cols, (D,), jnp.float32, math.log(0.6), math.log(1.6)))
    row_scale = jnp.exp(jax.random.uniform(key_rows, (TOKENS, 1), jnp.float32, math.log(0.5), math.log(2.0)))
    base = jnp.clip(jax.random.normal(key_base, (TOKENS, D), jnp.float32), -4.0, 4.0)
    return (row_scale * column_scale[None, :] * base).astype(jnp.bfloat16)


def with_ends(values, rng, smallest, high):
    spot = [jax.random.randint(jax.random.fold_in(rng, axis), (), 0, length) for axis, length in enumerate(values.shape)]
    main_axis = values.shape.index(max(values.shape))
    next_to = spot[:main_axis] + [(spot[main_axis] + 1) % values.shape[main_axis]] + spot[main_axis + 1:]
    return values.at[tuple(spot)].set(smallest).at[tuple(next_to)].set(high)


def block_scale(own_key, shape, cuts, smallest, top_value):
    loudness = 1.0
    for dim, parts in cuts:
        steps = jax.random.uniform(jax.random.fold_in(jax.random.fold_in(own_key, 6), dim), (parts,), jnp.float32, smallest / len(cuts), top_value / len(cuts))
        loudness = loudness * jnp.repeat(jnp.exp(steps), shape[dim] // parts).reshape((-1,) + (1,) * (len(shape) - 1 - dim))
    return loudness


def bell_draw(key, shape, scale, bound, pieces=(), kind=jnp.bfloat16):
    array = jax.random.normal(key, shape, jnp.float32) * scale
    if len(pieces) > 0:
        array = block_scale(key, shape, pieces, -0.22, 0.18) * array
    return jnp.clip(array, min=-bound, max=bound).astype(kind)


def setup_inputs(seed: int = 0) -> dict:
    keys = jax.random.split(jax.random.key(seed), 11)
    return {
        "layer_input": draw_layer_input(jax.random.fold_in(keys[10], 71), 0),
        "gate_pre": bell_draw(keys[1], (TOKENS, FF), 1.0, 5.0, ((0, 8), (1, 4))),
        "up_pre": bell_draw(keys[2], (TOKENS, FF), 1.0, 5.0, ((0, 8), (1, 4))),
        "hidden_cot": bell_draw(keys[3], (TOKENS, FF), 1.0, 6.0, ((0, 8), (1, 4))),
        "teacher_ids": with_ends(jax.random.randint(keys[4], (TOKENS,), 0, CLASSES), jax.random.fold_in(keys[4], 1), 0, CLASSES - 1).astype(jnp.int32),
        "adv_table": jnp.clip(jax.random.uniform(keys[5], (CLASSES,), jnp.float32, 0.25, 2.0), 0.25, 2.0),
        "gate_weight": bell_draw(keys[6], (D, FF), D ** -0.5, 0.09375, ((0, 8), (1, 4))),
        "up_weight": bell_draw(keys[7], (D, FF), D ** -0.5, 0.09375, ((0, 8), (1, 4))),
        "row_moments": jnp.clip(jnp.exp(math.log(0.5) - 2.3025851 * jax.random.uniform(keys[8], (2, D), jnp.float32) ** block_scale(keys[8], (2, D), ((1, 8),), -0.2, 0.2)), 0.05, 0.5),
        "col_moments": jnp.clip(jnp.exp(math.log(0.5) - 2.3025851 * jax.random.uniform(keys[9], (2, FF), jnp.float32) ** block_scale(keys[9], (2, FF), ((1, 4),), -0.2, 0.2)), 0.05, 0.5),
    }


decay_rate = 0.9
tanh_scale = math.sqrt(2.0 / math.pi)
cubic_term = 0.044715

def gelu_pair(pre_act):
    argument = tanh_scale * (pre_act + cubic_term * pre_act * pre_act * pre_act)
    tangent = jnp.tanh(argument)
    gelu_value = 0.5 * pre_act * (1.0 + tangent)
    gelu_slope = 0.5 * (1.0 + tangent) + 0.5 * pre_act * (1.0 - tangent * tangent) * tanh_scale * (1.0 + 3.0 * cubic_term * pre_act * pre_act)
    return (gelu_value, gelu_slope)

def reference(layer_input, gate_pre, up_pre, hidden_cot, teacher_ids, adv_table, gate_weight, up_weight, row_moments, col_moments):
    advantage = adv_table[teacher_ids]
    weighted = hidden_cot.astype(jnp.float32) * advantage[:, None]
    gelu_value, gelu_slope = gelu_pair(gate_pre.astype(jnp.float32))
    gate_grad = (weighted * up_pre.astype(jnp.float32) * gelu_slope).astype(jnp.bfloat16)
    up_grad = (weighted * gelu_value).astype(jnp.bfloat16)
    contract_last = (((1,), (1,)), ((), ()))
    input_grad = (lax.dot_general(gate_grad, gate_weight, contract_last, preferred_element_type=jnp.float32) + lax.dot_general(up_grad, up_weight, contract_last, preferred_element_type=jnp.float32)).astype(jnp.bfloat16)
    input_blocks = layer_input.reshape(N_DP, TOK_DEV, D)
    gate_blocks = gate_grad.reshape(N_DP, TOK_DEV, FF)
    up_blocks = up_grad.reshape(N_DP, TOK_DEV, FF)
    contract_first = (((0,), (0,)), ((), ()))

    def add_block(totals, blocks):
        input_block, gate_block, up_block = blocks
        gate_term = lax.dot_general(input_block, gate_block, contract_first, preferred_element_type=jnp.float32)
        up_term = lax.dot_general(input_block, up_block, contract_first, preferred_element_type=jnp.float32)
        gate_term = lax.optimization_barrier(gate_term.astype(jnp.bfloat16)).astype(jnp.float32)
        up_term = lax.optimization_barrier(up_term.astype(jnp.bfloat16)).astype(jnp.float32)
        return ((totals[0] + gate_term, totals[1] + up_term), None)
    zeros_block = jnp.zeros((D, FF), jnp.float32)
    (gate_sum, up_sum), unused = lax.scan(add_block, (zeros_block, zeros_block), (input_blocks, gate_blocks, up_blocks))
    grad_scale = 1.0 / math.sqrt(TOKENS)
    update_list = []
    row_list = []
    col_list = []
    for position, summed in enumerate((gate_sum, up_sum)):
        gradient = summed * grad_scale
        squares = gradient * gradient
        row_new = decay_rate * row_moments[position] + (1.0 - decay_rate) * lax.optimization_barrier(jnp.mean(squares, axis=1))
        col_new = decay_rate * col_moments[position] + (1.0 - decay_rate) * lax.optimization_barrier(jnp.mean(squares, axis=0))
        scaled = gradient / jnp.sqrt(row_new[:, None] * col_new[None, :])
        mean_square = jnp.mean(scaled * scaled)
        update_list.append(scaled / jnp.sqrt(mean_square + 1e-06))
        row_list.append(row_new)
        col_list.append(col_new)
    return (input_grad, update_list[0], update_list[1], jnp.stack(row_list), jnp.stack(col_list))
```

```python
import functools
import math

import jax
import jax.numpy as jnp
from jax import lax
from jax.experimental import pallas as pl
from jax.experimental.pallas import tpu as pltpu
from jax.sharding import PartitionSpec as P

decay_rate = 0.9
tanh_scale = math.sqrt(2.0 / math.pi)
cubic_term = 0.044715
f32 = jnp.float32
bf16 = jnp.bfloat16
AXES = ("dp", "mp")
GRID = (4, 2, 2, 2)


def gelu_pair(pre_act):
    argument = tanh_scale * (pre_act + cubic_term * pre_act * pre_act * pre_act)
    tangent = jnp.tanh(argument)
    gelu_value = 0.5 * pre_act * (1.0 + tangent)
    gelu_slope = 0.5 * (1.0 + tangent) + 0.5 * pre_act * (1.0 - tangent * tangent) * tanh_scale * (
        1.0 + 3.0 * cubic_term * pre_act * pre_act
    )
    return (gelu_value, gelu_slope)


def token_advantage(teacher_ids, adv_table):
    classes = adv_table.shape[0]
    class_hit = teacher_ids[:, None] == jnp.arange(classes, dtype=jnp.int32)[None, :]
    return jnp.sum(jnp.where(class_hit, adv_table[None, :], 0.0), axis=1)


def local_any(
    layer_input,
    gate_pre,
    up_pre,
    hidden_cot,
    teacher_ids,
    adv_table,
    gate_weight,
    up_weight,
    row_moments,
    col_moments,
):
    data_size = lax.axis_size("dp")
    model_size = lax.axis_size("mp")
    block_rows = gate_weight.shape[0]
    block_cols = gate_weight.shape[1]
    token_count = layer_input.shape[0]
    advantage = token_advantage(teacher_ids, adv_table)
    weighted = hidden_cot.astype(f32) * advantage[:, None]
    gelu_value, gelu_slope = gelu_pair(gate_pre.astype(f32))
    gate_grad = (weighted * up_pre.astype(f32) * gelu_slope).astype(bf16)
    up_grad = (weighted * gelu_value).astype(bf16)
    contract_last = (((1,), (1,)), ((), ()))
    contract_first = (((0,), (0,)), ((), ()))
    pieces = lax.all_gather((gate_weight, up_weight), "dp", axis=0, tiled=True)
    partial_sum = lax.dot_general(
        gate_grad, pieces[0], contract_last, preferred_element_type=f32
    ) + lax.dot_general(up_grad, pieces[1], contract_last, preferred_element_type=f32)
    input_grad = lax.psum_scatter(
        partial_sum.astype(bf16), "mp", scatter_dimension=1, tiled=True
    )
    grad_scale = 1.0 / math.sqrt(token_count * data_size)
    gate_term = lax.dot_general(layer_input, gate_grad, contract_first, preferred_element_type=f32)
    up_term = lax.dot_general(layer_input, up_grad, contract_first, preferred_element_type=f32)
    summed = lax.psum_scatter(
        jnp.concatenate([gate_term, up_term], axis=1).astype(bf16),
        "dp",
        scatter_dimension=0,
        tiled=True,
    ).astype(f32)
    grad_gate = summed[:, :block_cols] * grad_scale
    grad_up = summed[:, block_cols:] * grad_scale
    squares_gate = grad_gate * grad_gate
    squares_up = grad_up * grad_up
    row_local = jnp.stack([jnp.sum(squares_gate, axis=1), jnp.sum(squares_up, axis=1)])
    col_local = jnp.stack([jnp.sum(squares_gate, axis=0), jnp.sum(squares_up, axis=0)])
    row_total = lax.psum(row_local, "mp")
    col_total = lax.psum(col_local, "dp")
    new_rows = decay_rate * row_moments + (1.0 - decay_rate) * (
        row_total / (block_cols * model_size)
    )
    new_cols = decay_rate * col_moments + (1.0 - decay_rate) * (
        col_total / (block_rows * data_size)
    )
    scaled_gate = grad_gate / jnp.sqrt(new_rows[0][:, None] * new_cols[0][None, :])
    scaled_up = grad_up / jnp.sqrt(new_rows[1][:, None] * new_cols[1][None, :])
    square_sums = lax.psum(
        jnp.stack([jnp.sum(scaled_gate * scaled_gate), jnp.sum(scaled_up * scaled_up)]),
        ("dp", "mp"),
    )
    entry_count = block_rows * data_size * block_cols * model_size
    mean_square = square_sums / entry_count
    gate_update = scaled_gate / jnp.sqrt(mean_square[0] + 1e-06)
    up_update = scaled_up / jnp.sqrt(mean_square[1] + 1e-06)
    return (input_grad, gate_update, up_update, new_rows, new_cols)


def device_number(place):
    number = 0
    for coordinate, size in zip(place, GRID):
        number = number * size + coordinate
    return number


def pairs(target):
    out = []
    for z in range(GRID[0]):
        for x in range(GRID[1]):
            for y in range(GRID[2]):
                for c in range(GRID[3]):
                    place = target(z, x, y, c)
                    if place is not None:
                        out.append((device_number((z, x, y, c)), device_number(place)))
    return out


def flip_z(k):
    return pairs(lambda z, x, y, c: (z ^ k, x, y, c))


FLIP_X = pairs(lambda z, x, y, c: (z, 1 - x, y, c))
FLIP_Y = pairs(lambda z, x, y, c: (z, x, 1 - y, c))
FLIP_C = pairs(lambda z, x, y, c: (z, x, y, 1 - c))
MIDDLE = pairs(lambda z, x, y, c: (3 - z, x, y, c) if z in (1, 2) else None)
OUTWARD = pairs(lambda z, x, y, c: ({1: 0, 2: 3}[z], x, y, c) if z in (1, 2) else None)
HOME = pairs(lambda z, x, y, c: (z ^ (2 * y + c), x, z >> 1, z & 1))


def send(value, permutation):
    return lax.ppermute(value, AXES, permutation)


def front_kernel(ids_ref, table_ref, cot_ref, gate_ref, up_ref, gate_out, up_out):
    classes = table_ref.shape[1]
    ids = ids_ref[...]
    hit = ids == lax.broadcasted_iota(jnp.int32, (ids.shape[0], classes), 1)
    advantage = jnp.sum(jnp.where(hit, table_ref[...], 0.0), axis=1, keepdims=True)
    weighted = cot_ref[...].astype(f32) * advantage
    value, slope = gelu_pair(gate_ref[...].astype(f32))
    gate_out[...] = (weighted * up_ref[...].astype(f32) * slope).astype(bf16)
    up_out[...] = (weighted * value).astype(bf16)


def front(teacher_ids, adv_table, hidden_cot, gate_pre, up_pre, start, width):
    tokens = hidden_cot.shape[0]
    rows = 128
    first = start // width
    block = pl.BlockSpec((rows, width), lambda i: (i, first))
    out_block = pl.BlockSpec((rows, width), lambda i: (i, 0))
    shape = jax.ShapeDtypeStruct((tokens, width), bf16)
    return pl.pallas_call(
        front_kernel,
        grid=(tokens // rows,),
        in_specs=[
            pl.BlockSpec((rows, 1), lambda i: (i, 0)),
            pl.BlockSpec((1, adv_table.shape[0]), lambda i: (0, 0)),
            block,
            block,
            block,
        ],
        out_specs=[out_block, out_block],
        out_shape=[shape, shape],
        cost_estimate=pl.CostEstimate(
            flops=60 * tokens * width, bytes_accessed=10 * tokens * width, transcendentals=0
        ),
    )(teacher_ids[:, None], adv_table[None, :], hidden_cot, gate_pre, up_pre)


def gather_column(own):
    near = send(own, flip_z(1))
    across_own = send(own, MIDDLE)
    across_near = send(near, MIDDLE)
    out_own = send(across_own, OUTWARD)
    out_near = send(across_near, OUTWARD)
    return jnp.concatenate([own, near, across_near + out_own, across_own + out_near], axis=0)


def dot_first(a, b):
    return lax.dot_general(a, b, (((0,), (0,)), ((), ())), preferred_element_type=f32)


def dot_last(a, b):
    return lax.dot_general(a, b, (((1,), (1,)), ((), ())), preferred_element_type=f32)


def sum_over(value, permutations):
    for permutation in permutations:
        value = value + send(value, permutation)
    return value


OVER_DP = (FLIP_X, flip_z(1), flip_z(2))
OVER_MP = (FLIP_C, FLIP_Y)


def local_block(
    layer_input,
    gate_pre,
    up_pre,
    hidden_cot,
    teacher_ids,
    adv_table,
    gate_weight,
    up_weight,
    row_moments,
    col_moments,
):
    data_size = lax.axis_size("dp")
    model_size = lax.axis_size("mp")
    rows, cols = gate_weight.shape
    tokens = layer_input.shape[0]
    dp = lax.axis_index("dp")
    m = lax.axis_index("mp")
    z, x = dp // 2, dp % 2
    y, c = m // 2, m % 2
    piece_rows = tokens // model_size
    plane = 2 * rows

    def input_columns(array, k):
        base = (z ^ k) * plane
        size = array.shape[0]
        return jnp.concatenate(
            [
                lax.dynamic_slice(array, (0, base + x * rows), (size, rows)),
                lax.dynamic_slice(array, (0, base + (1 - x) * rows), (size, rows)),
            ],
            axis=1,
        )

    mine = lax.dynamic_slice(layer_input, (m * piece_rows, 0), (piece_rows, layer_input.shape[1]))
    piece = jnp.stack([send(input_columns(mine, k), flip_z(k)) for k in (1, 2, 3)])
    piece_c = send(piece, FLIP_C)
    piece_y = send(piece, FLIP_Y)
    piece_yc = send(piece_y, FLIP_C)
    far = jnp.zeros((3, model_size, piece_rows, plane), bf16)
    for part, place in ((piece, m), (piece_c, m ^ 1), (piece_y, m ^ 2), (piece_yc, m ^ 3)):
        far = lax.dynamic_update_slice(far, part[:, None], (0, place, 0, 0))
    inputs = jnp.concatenate(
        [input_columns(layer_input, 0), far.reshape(3 * tokens, plane)], axis=0
    )

    def plane_rows(weight):
        other = send(weight, FLIP_X)
        both = jnp.zeros((plane, cols), bf16)
        both = lax.dynamic_update_slice(both, weight, (x * rows, 0))
        return lax.dynamic_update_slice(both, other, ((1 - x) * rows, 0))

    weights = (plane_rows(gate_weight), plane_rows(up_weight))

    width = cols // 2
    grads = [
        front(teacher_ids, adv_table, hidden_cot, gate_pre, up_pre, start, width)
        for start in range(0, cols, width)
    ]
    grad_scale = 1.0 / math.sqrt(tokens * data_size)
    partial_input = None
    sums = []
    for k in range(2):
        chunks = []
        for position, start in enumerate(range(0, cols, width)):
            gathered = gather_column(grads[position][k])
            away = dot_first(inputs[:, rows:], gathered).astype(bf16)
            keep = dot_first(inputs[:, :rows], gathered)
            chunks.append((keep + send(away, FLIP_X).astype(f32)) * grad_scale)
            term = dot_last(gathered, weights[k][:, start : start + width])
            partial_input = term if partial_input is None else partial_input + term
        sums.append(chunks)

    blocks = partial_input.reshape(2, 2, tokens, plane)
    keep = jnp.where(c == 0, blocks[:, 0], blocks[:, 1])
    away = jnp.where(c == 0, blocks[:, 1], blocks[:, 0]).astype(bf16)
    blocks = keep + send(away, FLIP_C).astype(f32)
    keep = jnp.where(y == 0, blocks[0], blocks[1])
    away = jnp.where(y == 0, blocks[1], blocks[0]).astype(bf16)
    block = (keep + send(away, FLIP_Y).astype(f32)).astype(bf16)
    input_grad = send(block, HOME)

    entry_count = rows * data_size * cols * model_size
    updates, new_rows, new_cols = [], [], []
    for k, chunks in enumerate(sums):
        squares = [chunk * chunk for chunk in chunks]
        row_total = sum_over(sum(jnp.sum(s, axis=1) for s in squares), OVER_MP)
        row = decay_rate * row_moments[k] + (1.0 - decay_rate) * (
            row_total / (cols * model_size)
        )
        col_total = sum_over(
            jnp.concatenate([jnp.sum(s, axis=0) for s in squares]), OVER_DP
        )
        col = decay_rate * col_moments[k] + (1.0 - decay_rate) * (
            col_total / (rows * data_size)
        )
        row_factor = lax.rsqrt(row)[:, None]
        col_factor = lax.rsqrt(col)[None, :]
        scaled = [
            chunk * row_factor * col_factor[:, i * width : (i + 1) * width]
            for i, chunk in enumerate(chunks)
        ]
        square_sum = sum_over(
            jnp.broadcast_to(sum(jnp.sum(s * s) for s in scaled), (128,)), OVER_MP + OVER_DP
        )[0]
        factor = lax.rsqrt(square_sum / entry_count + 1e-06)
        updates.append(jnp.concatenate([s * factor for s in scaled], axis=1))
        new_rows.append(row)
        new_cols.append(col)
    return (input_grad, updates[0], updates[1], jnp.stack(new_rows), jnp.stack(new_cols))


def solution(mesh):
    in_specs = (
        P("dp", None),
        P("dp", "mp"),
        P("dp", "mp"),
        P("dp", "mp"),
        P("dp"),
        P(),
        P("dp", "mp"),
        P("dp", "mp"),
        P(None, "dp"),
        P(None, "mp"),
    )
    out_specs = (P("dp", "mp"), P("dp", "mp"), P("dp", "mp"), P(None, "dp"), P(None, "mp"))
    fits = (mesh.shape["dp"], mesh.shape["mp"]) == (GRID[0] * GRID[1], GRID[2] * GRID[3])
    local = local_block if fits else local_any
    return jax.shard_map(local, mesh=mesh, in_specs=in_specs, out_specs=out_specs, check_vma=False)
```

```python
import functools
import math

import jax
import jax.numpy as jnp
from jax import lax
from jax.experimental import pallas as pl
from jax.experimental.pallas import tpu as pltpu
from jax.sharding import PartitionSpec as P

decay_rate = 0.9
tanh_scale = math.sqrt(2.0 / math.pi)
cubic_term = 0.044715
f32 = jnp.float32
bf16 = jnp.bfloat16
AXES = ("dp", "mp")
GRID = (4, 2, 2, 2)


def gelu_pair(pre_act):
    argument = tanh_scale * (pre_act + cubic_term * pre_act * pre_act * pre_act)
    tangent = jnp.tanh(argument)
    gelu_value = 0.5 * pre_act * (1.0 + tangent)
    gelu_slope = 0.5 * (1.0 + tangent) + 0.5 * pre_act * (1.0 - tangent * tangent) * tanh_scale * (
        1.0 + 3.0 * cubic_term * pre_act * pre_act
    )
    return (gelu_value, gelu_slope)


def token_advantage(teacher_ids, adv_table):
    classes = adv_table.shape[0]
    class_hit = teacher_ids[:, None] == jnp.arange(classes, dtype=jnp.int32)[None, :]
    return jnp.sum(jnp.where(class_hit, adv_table[None, :], 0.0), axis=1)


def local_any(
    layer_input,
    gate_pre,
    up_pre,
    hidden_cot,
    teacher_ids,
    adv_table,
    gate_weight,
    up_weight,
    row_moments,
    col_moments,
):
    data_size = lax.axis_size("dp")
    model_size = lax.axis_size("mp")
    block_rows = gate_weight.shape[0]
    block_cols = gate_weight.shape[1]
    token_count = layer_input.shape[0]
    advantage = token_advantage(teacher_ids, adv_table)
    weighted = hidden_cot.astype(f32) * advantage[:, None]
    gelu_value, gelu_slope = gelu_pair(gate_pre.astype(f32))
    gate_grad = (weighted * up_pre.astype(f32) * gelu_slope).astype(bf16)
    up_grad = (weighted * gelu_value).astype(bf16)
    contract_last = (((1,), (1,)), ((), ()))
    contract_first = (((0,), (0,)), ((), ()))
    pieces = lax.all_gather((gate_weight, up_weight), "dp", axis=0, tiled=True)
    partial_sum = lax.dot_general(
        gate_grad, pieces[0], contract_last, preferred_element_type=f32
    ) + lax.dot_general(up_grad, pieces[1], contract_last, preferred_element_type=f32)
    input_grad = lax.psum_scatter(
        partial_sum.astype(bf16), "mp", scatter_dimension=1, tiled=True
    )
    grad_scale = 1.0 / math.sqrt(token_count * data_size)
    gate_term = lax.dot_general(layer_input, gate_grad, contract_first, preferred_element_type=f32)
    up_term = lax.dot_general(layer_input, up_grad, contract_first, preferred_element_type=f32)
    summed = lax.psum_scatter(
        jnp.concatenate([gate_term, up_term], axis=1).astype(bf16),
        "dp",
        scatter_dimension=0,
        tiled=True,
    ).astype(f32)
    grad_gate = summed[:, :block_cols] * grad_scale
    grad_up = summed[:, block_cols:] * grad_scale
    squares_gate = grad_gate * grad_gate
    squares_up = grad_up * grad_up
    row_local = jnp.stack([jnp.sum(squares_gate, axis=1), jnp.sum(squares_up, axis=1)])
    col_local = jnp.stack([jnp.sum(squares_gate, axis=0), jnp.sum(squares_up, axis=0)])
    row_total = lax.psum(row_local, "mp")
    col_total = lax.psum(col_local, "dp")
    new_rows = decay_rate * row_moments + (1.0 - decay_rate) * (
        row_total / (block_cols * model_size)
    )
    new_cols = decay_rate * col_moments + (1.0 - decay_rate) * (
        col_total / (block_rows * data_size)
    )
    scaled_gate = grad_gate / jnp.sqrt(new_rows[0][:, None] * new_cols[0][None, :])
    scaled_up = grad_up / jnp.sqrt(new_rows[1][:, None] * new_cols[1][None, :])
    square_sums = lax.psum(
        jnp.stack([jnp.sum(scaled_gate * scaled_gate), jnp.sum(scaled_up * scaled_up)]),
        ("dp", "mp"),
    )
    entry_count = block_rows * data_size * block_cols * model_size
    mean_square = square_sums / entry_count
    gate_update = scaled_gate / jnp.sqrt(mean_square[0] + 1e-06)
    up_update = scaled_up / jnp.sqrt(mean_square[1] + 1e-06)
    return (input_grad, gate_update, up_update, new_rows, new_cols)


def device_number(place):
    number = 0
    for coordinate, size in zip(place, GRID):
        number = number * size + coordinate
    return number


def pairs(target):
    out = []
    for z in range(GRID[0]):
        for x in range(GRID[1]):
            for y in range(GRID[2]):
                for c in range(GRID[3]):
                    place = target(z, x, y, c)
                    if place is not None:
                        out.append((device_number((z, x, y, c)), device_number(place)))
    return out


def flip_z(k):
    return pairs(lambda z, x, y, c: (z ^ k, x, y, c))


FLIP_X = pairs(lambda z, x, y, c: (z, 1 - x, y, c))
FLIP_Y = pairs(lambda z, x, y, c: (z, x, 1 - y, c))
FLIP_C = pairs(lambda z, x, y, c: (z, x, y, 1 - c))
MIDDLE = pairs(lambda z, x, y, c: (3 - z, x, y, c) if z in (1, 2) else None)
OUTWARD = pairs(lambda z, x, y, c: ({1: 0, 2: 3}[z], x, y, c) if z in (1, 2) else None)
INWARD = pairs(lambda z, x, y, c: ({0: 1, 3: 2}[z], x, y, c) if z in (0, 3) else None)


def home(first, half):
    return pairs(lambda z, x, y, c: (z ^ (first + c), x, z >> 1, z & 1) if y == half else None)


def send(value, permutation):
    return lax.ppermute(value, AXES, permutation)


def tie(*values):
    return lax.optimization_barrier(values)


def advantage_of(ids_ref, table_ref):
    ids = ids_ref[...]
    hit = ids == lax.broadcasted_iota(jnp.int32, (ids.shape[0], table_ref.shape[1]), 1)
    return jnp.sum(jnp.where(hit, table_ref[...], 0.0), axis=1, keepdims=True)


def gate_kernel(ids_ref, table_ref, cot_ref, gate_ref, up_ref, out_ref):
    weighted = cot_ref[...].astype(f32) * advantage_of(ids_ref, table_ref)
    slope = gelu_pair(gate_ref[...].astype(f32))[1]
    out_ref[...] = (weighted * up_ref[...].astype(f32) * slope).astype(bf16)


def up_kernel(ids_ref, table_ref, cot_ref, gate_ref, out_ref):
    weighted = cot_ref[...].astype(f32) * advantage_of(ids_ref, table_ref)
    out_ref[...] = (weighted * gelu_pair(gate_ref[...].astype(f32))[0]).astype(bf16)


def front(kernel, teacher_ids, adv_table, arrays):
    tokens, cols = arrays[0].shape
    rows = 128
    block = pl.BlockSpec((rows, cols), lambda i: (i, 0))
    return pl.pallas_call(
        kernel,
        grid=(tokens // rows,),
        in_specs=[
            pl.BlockSpec((rows, 1), lambda i: (i, 0)),
            pl.BlockSpec((1, adv_table.shape[0]), lambda i: (0, 0)),
        ]
        + [block] * len(arrays),
        out_specs=block,
        out_shape=jax.ShapeDtypeStruct((tokens, cols), bf16),
        cost_estimate=pl.CostEstimate(
            flops=40 * tokens * cols, bytes_accessed=8 * tokens * cols, transcendentals=0
        ),
    )(teacher_ids[:, None], adv_table[None, :], *arrays)


def dot_first(a, b):
    return lax.dot_general(a, b, (((0,), (0,)), ((), ())), preferred_element_type=f32)


def dot_last(a, b):
    return lax.dot_general(a, b, (((1,), (1,)), ((), ())), preferred_element_type=f32)


def sum_over(value, permutations):
    for permutation in permutations:
        value = value + send(value, permutation)
    return value


OVER_DP = (FLIP_X, flip_z(1), flip_z(2))
OVER_MP = (FLIP_C, FLIP_Y)


def local_block(
    layer_input,
    gate_pre,
    up_pre,
    hidden_cot,
    teacher_ids,
    adv_table,
    gate_weight,
    up_weight,
    row_moments,
    col_moments,
):
    data_size = lax.axis_size("dp")
    model_size = lax.axis_size("mp")
    rows, cols = gate_weight.shape
    tokens = layer_input.shape[0]
    dp = lax.axis_index("dp")
    m = lax.axis_index("mp")
    z, x = dp // 2, dp % 2
    y, c = m // 2, m % 2
    piece_rows = tokens // model_size
    plane = 2 * rows
    first = cols * 7 // 10 // 128 * 128
    grad_scale = 1.0 / math.sqrt(tokens * data_size)

    def input_columns(array, k):
        base = (z ^ k) * plane
        size = array.shape[0]
        return jnp.concatenate(
            [
                lax.dynamic_slice(array, (0, base + x * rows), (size, rows)),
                lax.dynamic_slice(array, (0, base + (1 - x) * rows), (size, rows)),
            ],
            axis=1,
        )

    def plane_rows(own, other):
        both = jnp.zeros((plane, cols), bf16)
        both = lax.dynamic_update_slice(both, own, (x * rows, 0))
        return lax.dynamic_update_slice(both, other, ((1 - x) * rows, 0))

    def over_core(first, second):
        keep = jnp.where(c == 0, first, second)
        away = jnp.where(c == 0, second, first).astype(bf16)
        return keep, away

    def over_y(block):
        part = tokens // 2
        keep = lax.dynamic_slice(block, (y * part, 0), (part, plane))
        away = lax.dynamic_slice(block, ((1 - y) * part, 0), (part, plane)).astype(bf16)
        return keep, away

    first_columns, second_columns = slice(0, first), slice(first, cols)

    def gradient(keep, recv):
        return (keep + recv.astype(f32)) * grad_scale

    def products(block, part):
        return dot_first(part[:, rows:], block), dot_first(part[:, :rows], block)

    mine = lax.dynamic_slice(layer_input, (m * piece_rows, 0), (piece_rows, layer_input.shape[1]))
    piece = [send(input_columns(mine, k), flip_z(k)) for k in (1, 2, 3)]
    g = front(gate_kernel, teacher_ids, adv_table, (hidden_cot, gate_pre, up_pre))
    g, gate_pre, hidden_cot = tie(g, gate_pre, hidden_cot)
    g_near = send(g, flip_z(1))
    g_over = send(g, MIDDLE)
    u = front(up_kernel, teacher_ids, adv_table, (hidden_cot, gate_pre))
    piece, u, gate_weight = tie(piece, u, gate_weight)

    u_near = send(u, flip_z(1))
    u_over = send(u, MIDDLE)
    gate_other = send(gate_weight, FLIP_X)
    g_near, g_over = tie(g_near, g_over)

    g_far = send(g_over, OUTWARD)
    g_near_over = send(g_near, MIDDLE)
    u_near, u_over, gate_other, up_weight, piece = tie(u_near, u_over, gate_other, up_weight, piece)

    u_far = send(u_over, OUTWARD)
    u_near_over = send(u_near, MIDDLE)
    up_other = send(up_weight, FLIP_X)
    gate_rows = plane_rows(gate_weight, gate_other)
    early = dot_last(jnp.concatenate([g, g_near], axis=0), gate_rows)
    g_far, g_near_over, piece, early = tie(g_far, g_near_over, piece, early)

    g_farthest = send(g_near_over, OUTWARD)
    piece = jnp.stack(piece)
    piece_y = send(piece, FLIP_Y)
    g_third = g_near_over + g_far
    u_far, u_near_over, up_other, piece_y, g_third = tie(u_far, u_near_over, up_other, piece_y, g_third)

    u_farthest = [send(u_near_over[:, columns], OUTWARD) for columns in (first_columns, second_columns)]
    pieces = jnp.stack([piece, piece_y])
    pieces_c = send(pieces, FLIP_C)
    up_rows = plane_rows(up_weight, up_other)
    u_third = u_near_over + u_far
    early = early + dot_last(jnp.concatenate([u, u_near], axis=0), up_rows)
    third = dot_last(g_third, gate_rows) + dot_last(u_third, up_rows)
    pieces_c, early, third, g_third, u_third = tie(pieces_c, early, third, g_third, u_third)

    early_keep, early_away = over_core(early[:tokens], early[tokens:])
    early_recv = send(early_away, FLIP_C)
    far = jnp.zeros((3, model_size, piece_rows, plane), bf16)
    for part, place in ((pieces[0], m), (pieces_c[0], m ^ 1), (pieces[1], m ^ 2), (pieces_c[1], m ^ 3)):
        far = lax.dynamic_update_slice(far, part[:, None], (0, place, 0, 0))
    near_inputs = jnp.concatenate([input_columns(layer_input, 0), far[:2].reshape(2 * tokens, plane)])
    far_inputs = far[2].reshape(tokens, plane)
    g_away, g_keep = products(jnp.concatenate([g, g_near, g_third], axis=0), near_inputs)
    g_away, g_keep, early_keep, early_recv, g_farthest = tie(
        g_away, g_keep, early_keep, early_recv, g_farthest
    )

    g_last = g_over + g_farthest
    last_away, last_keep = products(g_last, far_inputs)
    g_recv = send((g_away + last_away).astype(bf16), FLIP_X)
    g_keep = g_keep + last_keep
    early_keep, early_away = over_y(early_keep + early_recv.astype(f32))
    early_recv = send(early_away, FLIP_Y)
    last = dot_last(g_last, gate_rows)
    u_away, u_keep = products(jnp.concatenate([u, u_near, u_third], axis=0), near_inputs)
    last, u_away, u_keep, early_keep, early_recv, g_keep, u_farthest[0] = tie(
        last, u_away, u_keep, early_keep, early_recv, g_keep, u_farthest[0]
    )

    block = u_over[:, first_columns] + u_farthest[0]
    last_away, last_keep = products(block, far_inputs)
    first_recv = send((u_away[:, first_columns] + last_away).astype(bf16), FLIP_X)
    first_keep = u_keep[:, first_columns] + last_keep
    early_sum = (early_keep + early_recv.astype(f32)).astype(bf16)
    early_home = [send(early_sum, home(0, h)) for h in range(2)]
    last = last + dot_last(block, up_rows[:, first_columns])
    last, first_keep, u_farthest[1] = tie(last, first_keep, u_farthest[1])

    block = u_over[:, second_columns] + u_farthest[1]
    last = last + dot_last(block, up_rows[:, second_columns])
    late_keep, late_away = over_core(third, last)
    late_away, late_keep, block, g_recv = tie(late_away, late_keep, block, g_recv)
    late_recv = send(late_away, FLIP_C)
    last_away, last_keep = products(block, far_inputs)
    second_recv = send((u_away[:, second_columns] + last_away).astype(bf16), FLIP_X)
    second_keep = u_keep[:, second_columns] + last_keep
    gate_gradient = gradient(g_keep, g_recv)
    gate_row = jnp.sum(gate_gradient * gate_gradient, axis=1)
    gate_col = jnp.sum(gate_gradient * gate_gradient, axis=0)
    late_keep, late_away = over_y(late_keep + late_recv.astype(f32))
    late_keep, late_away, second_recv, second_keep, gate_row, gate_col, gate_gradient, early_home = tie(
        late_keep, late_away, second_recv, second_keep, gate_row, gate_col, gate_gradient, early_home
    )

    entry_count = rows * data_size * cols * model_size
    up_gradient = jnp.concatenate(
        [gradient(first_keep, first_recv), gradient(second_keep, second_recv)], axis=1
    )
    gradients = (gate_gradient, up_gradient)
    squares = up_gradient * up_gradient
    row_total = sum_over(jnp.stack([gate_row, jnp.sum(squares, axis=1)]), OVER_MP)
    row_total, late_away = tie(row_total, late_away)
    late_recv = send(late_away, FLIP_Y)
    new_rows = decay_rate * row_moments + (1.0 - decay_rate) * (row_total / (cols * model_size))
    inverse = 1.0 / new_rows
    column_sums = jnp.concatenate(
        [gate_col, jnp.sum(squares, axis=0)]
        + [jnp.sum(v * v * inverse[k][:, None], axis=0) for k, v in enumerate(gradients)]
    )
    column_sums = sum_over(column_sums, OVER_DP).reshape(2, 2, cols)
    column_sums, late_recv = tie(column_sums, late_recv)
    late_sum = (late_keep + late_recv.astype(f32)).astype(bf16)
    input_grad = jnp.concatenate(
        [early_home[h] + send(late_sum, home(2, h)) for h in range(2)], axis=0
    )
    new_cols = decay_rate * col_moments + (1.0 - decay_rate) * (
        column_sums[0] / (rows * data_size)
    )
    square_sums = jnp.sum(column_sums[1] / new_cols, axis=1)
    square_sums = sum_over(jnp.broadcast_to(square_sums[:, None], (2, 128)), OVER_MP)[:, :1]
    row_factor = lax.rsqrt(new_rows) * lax.rsqrt(square_sums / entry_count + 1e-06)
    col_factor = lax.rsqrt(new_cols)
    updates = [
        v * row_factor[k][:, None] * col_factor[k][None, :] for k, v in enumerate(gradients)
    ]
    return input_grad, updates[0], updates[1], new_rows, new_cols


def solution(mesh):
    in_specs = (
        P("dp", None),
        P("dp", "mp"),
        P("dp", "mp"),
        P("dp", "mp"),
        P("dp"),
        P(),
        P("dp", "mp"),
        P("dp", "mp"),
        P(None, "dp"),
        P(None, "mp"),
    )
    out_specs = (P("dp", "mp"), P("dp", "mp"), P("dp", "mp"), P(None, "dp"), P(None, "mp"))
    fits = (mesh.shape["dp"], mesh.shape["mp"]) == (GRID[0] * GRID[1], GRID[2] * GRID[3])
    local = local_block if fits else local_any
    return jax.shard_map(local, mesh=mesh, in_specs=in_specs, out_specs=out_specs, check_vma=False)
```

```python
import functools
import math

import jax
import jax.numpy as jnp
from jax import lax
from jax.experimental import pallas as pl
from jax.experimental.pallas import tpu as pltpu
from jax.sharding import PartitionSpec as P

decay_rate = 0.9
tanh_scale = math.sqrt(2.0 / math.pi)
cubic_term = 0.044715
f32 = jnp.float32
bf16 = jnp.bfloat16
AXES = ("dp", "mp")
GRID = (4, 2, 2, 2)


def gelu_pair(pre_act):
    argument = tanh_scale * (pre_act + cubic_term * pre_act * pre_act * pre_act)
    tangent = jnp.tanh(argument)
    gelu_value = 0.5 * pre_act * (1.0 + tangent)
    gelu_slope = 0.5 * (1.0 + tangent) + 0.5 * pre_act * (1.0 - tangent * tangent) * tanh_scale * (
        1.0 + 3.0 * cubic_term * pre_act * pre_act
    )
    return (gelu_value, gelu_slope)


def token_advantage(teacher_ids, adv_table):
    classes = adv_table.shape[0]
    class_hit = teacher_ids[:, None] == jnp.arange(classes, dtype=jnp.int32)[None, :]
    return jnp.sum(jnp.where(class_hit, adv_table[None, :], 0.0), axis=1)


def local_any(
    layer_input,
    gate_pre,
    up_pre,
    hidden_cot,
    teacher_ids,
    adv_table,
    gate_weight,
    up_weight,
    row_moments,
    col_moments,
):
    data_size = lax.axis_size("dp")
    model_size = lax.axis_size("mp")
    block_rows = gate_weight.shape[0]
    block_cols = gate_weight.shape[1]
    token_count = layer_input.shape[0]
    advantage = token_advantage(teacher_ids, adv_table)
    weighted = hidden_cot.astype(f32) * advantage[:, None]
    gelu_value, gelu_slope = gelu_pair(gate_pre.astype(f32))
    gate_grad = (weighted * up_pre.astype(f32) * gelu_slope).astype(bf16)
    up_grad = (weighted * gelu_value).astype(bf16)
    contract_last = (((1,), (1,)), ((), ()))
    contract_first = (((0,), (0,)), ((), ()))
    pieces = lax.all_gather((gate_weight, up_weight), "dp", axis=0, tiled=True)
    partial_sum = lax.dot_general(
        gate_grad, pieces[0], contract_last, preferred_element_type=f32
    ) + lax.dot_general(up_grad, pieces[1], contract_last, preferred_element_type=f32)
    input_grad = lax.psum_scatter(
        partial_sum.astype(bf16), "mp", scatter_dimension=1, tiled=True
    )
    grad_scale = 1.0 / math.sqrt(token_count * data_size)
    gate_term = lax.dot_general(layer_input, gate_grad, contract_first, preferred_element_type=f32)
    up_term = lax.dot_general(layer_input, up_grad, contract_first, preferred_element_type=f32)
    summed = lax.psum_scatter(
        jnp.concatenate([gate_term, up_term], axis=1).astype(bf16),
        "dp",
        scatter_dimension=0,
        tiled=True,
    ).astype(f32)
    grad_gate = summed[:, :block_cols] * grad_scale
    grad_up = summed[:, block_cols:] * grad_scale
    squares_gate = grad_gate * grad_gate
    squares_up = grad_up * grad_up
    row_local = jnp.stack([jnp.sum(squares_gate, axis=1), jnp.sum(squares_up, axis=1)])
    col_local = jnp.stack([jnp.sum(squares_gate, axis=0), jnp.sum(squares_up, axis=0)])
    row_total = lax.psum(row_local, "mp")
    col_total = lax.psum(col_local, "dp")
    new_rows = decay_rate * row_moments + (1.0 - decay_rate) * (
        row_total / (block_cols * model_size)
    )
    new_cols = decay_rate * col_moments + (1.0 - decay_rate) * (
        col_total / (block_rows * data_size)
    )
    scaled_gate = grad_gate / jnp.sqrt(new_rows[0][:, None] * new_cols[0][None, :])
    scaled_up = grad_up / jnp.sqrt(new_rows[1][:, None] * new_cols[1][None, :])
    square_sums = lax.psum(
        jnp.stack([jnp.sum(scaled_gate * scaled_gate), jnp.sum(scaled_up * scaled_up)]),
        ("dp", "mp"),
    )
    entry_count = block_rows * data_size * block_cols * model_size
    mean_square = square_sums / entry_count
    gate_update = scaled_gate / jnp.sqrt(mean_square[0] + 1e-06)
    up_update = scaled_up / jnp.sqrt(mean_square[1] + 1e-06)
    return (input_grad, gate_update, up_update, new_rows, new_cols)


def device_number(place):
    number = 0
    for coordinate, size in zip(place, GRID):
        number = number * size + coordinate
    return number


def pairs(target):
    out = []
    for z in range(GRID[0]):
        for x in range(GRID[1]):
            for y in range(GRID[2]):
                for c in range(GRID[3]):
                    place = target(z, x, y, c)
                    if place is not None:
                        out.append((device_number((z, x, y, c)), device_number(place)))
    return out


def flip_z(k):
    return pairs(lambda z, x, y, c: (z ^ k, x, y, c))


FLIP_X = pairs(lambda z, x, y, c: (z, 1 - x, y, c))
FLIP_Y = pairs(lambda z, x, y, c: (z, x, 1 - y, c))
FLIP_C = pairs(lambda z, x, y, c: (z, x, y, 1 - c))
MIDDLE = pairs(lambda z, x, y, c: (3 - z, x, y, c) if z in (1, 2) else None)
OUTWARD = pairs(lambda z, x, y, c: ({1: 0, 2: 3}[z], x, y, c) if z in (1, 2) else None)
INWARD = pairs(lambda z, x, y, c: ({0: 1, 3: 2}[z], x, y, c) if z in (0, 3) else None)


def home(first, half):
    return pairs(lambda z, x, y, c: (z ^ (first + c), x, z >> 1, z & 1) if y == half else None)


def send(value, permutation):
    return lax.ppermute(value, AXES, permutation)


def tie(*values):
    return lax.optimization_barrier(values)


def advantage_of(ids_ref, table_ref):
    ids = ids_ref[...]
    hit = ids == lax.broadcasted_iota(jnp.int32, (ids.shape[0], table_ref.shape[1]), 1)
    return jnp.sum(jnp.where(hit, table_ref[...], 0.0), axis=1, keepdims=True)


def gate_kernel(ids_ref, table_ref, cot_ref, gate_ref, up_ref, out_ref):
    weighted = cot_ref[...].astype(f32) * advantage_of(ids_ref, table_ref)
    slope = gelu_pair(gate_ref[...].astype(f32))[1]
    out_ref[...] = (weighted * up_ref[...].astype(f32) * slope).astype(bf16)


def up_kernel(ids_ref, table_ref, cot_ref, gate_ref, out_ref):
    weighted = cot_ref[...].astype(f32) * advantage_of(ids_ref, table_ref)
    out_ref[...] = (weighted * gelu_pair(gate_ref[...].astype(f32))[0]).astype(bf16)


def front(kernel, teacher_ids, adv_table, arrays):
    tokens, cols = arrays[0].shape
    rows = 128
    block = pl.BlockSpec((rows, cols), lambda i: (i, 0))
    return pl.pallas_call(
        kernel,
        grid=(tokens // rows,),
        in_specs=[
            pl.BlockSpec((rows, 1), lambda i: (i, 0)),
            pl.BlockSpec((1, adv_table.shape[0]), lambda i: (0, 0)),
        ]
        + [block] * len(arrays),
        out_specs=block,
        out_shape=jax.ShapeDtypeStruct((tokens, cols), bf16),
        cost_estimate=pl.CostEstimate(
            flops=tokens * cols, bytes_accessed=tokens * cols, transcendentals=0
        ),
    )(teacher_ids[:, None], adv_table[None, :], *arrays)


def dot_first(a, b):
    return lax.dot_general(a, b, (((0,), (0,)), ((), ())), preferred_element_type=f32)


def dot_last(a, b):
    return lax.dot_general(a, b, (((1,), (1,)), ((), ())), preferred_element_type=f32)


def sum_over(value, permutations):
    for permutation in permutations:
        value = value + send(value, permutation)
    return value


OVER_DP = (FLIP_X, flip_z(1), flip_z(2))
OVER_MP = (FLIP_C, FLIP_Y)


def local_block(
    layer_input,
    gate_pre,
    up_pre,
    hidden_cot,
    teacher_ids,
    adv_table,
    gate_weight,
    up_weight,
    row_moments,
    col_moments,
):
    data_size = lax.axis_size("dp")
    model_size = lax.axis_size("mp")
    rows, cols = gate_weight.shape
    tokens = layer_input.shape[0]
    dp = lax.axis_index("dp")
    m = lax.axis_index("mp")
    z, x = dp // 2, dp % 2
    y, c = m // 2, m % 2
    piece_rows = tokens // model_size
    plane = 2 * rows
    grad_scale = 1.0 / math.sqrt(tokens * data_size)

    def plane_rows(own, other):
        both = jnp.zeros((plane, cols), bf16)
        both = lax.dynamic_update_slice(both, own, (x * rows, 0))
        return lax.dynamic_update_slice(both, other, ((1 - x) * rows, 0))

    def over_core(first, second):
        keep = jnp.where(c == 0, first, second)
        away = jnp.where(c == 0, second, first).astype(bf16)
        return keep, away

    def over_y(block):
        part = tokens // 2
        keep = lax.dynamic_slice(block, (y * part, 0), (part, plane))
        away = lax.dynamic_slice(block, ((1 - y) * part, 0), (part, plane)).astype(bf16)
        return keep, away

    def gradient(keep, recv):
        return (keep + recv.astype(f32)) * grad_scale

    mine = lax.dynamic_slice(layer_input, (m * piece_rows, 0), (piece_rows, layer_input.shape[1]))
    piece = [
        send(lax.dynamic_slice(mine, (0, (z ^ k) * plane), (piece_rows, plane)), flip_z(k))
        for k in (1, 2, 3)
    ]
    gate_other = send(gate_weight, FLIP_X)
    g = front(gate_kernel, teacher_ids, adv_table, (hidden_cot, gate_pre, up_pre))
    u = front(up_kernel, teacher_ids, adv_table, (hidden_cot, gate_pre))
    piece, g, u, gate_other, up_weight = tie(piece, g, u, gate_other, up_weight)

    g_near = send(g, flip_z(1))
    g_over = send(g, MIDDLE)
    u_near = send(u, flip_z(1))
    u_over = send(u, MIDDLE)
    up_other = send(up_weight, FLIP_X)
    piece = jnp.stack(piece)
    g_near, g_over, up_other, piece = tie(g_near, g_over, up_other, piece)

    g_far = send(g_over, OUTWARD)
    g_near_over = send(g_near, MIDDLE)
    piece_y = send(piece, FLIP_Y)
    gate_rows = plane_rows(gate_weight, gate_other)
    up_rows = plane_rows(up_weight, up_other)
    u_near, u_over, gate_rows, up_rows, piece, piece_y = tie(
        u_near, u_over, gate_rows, up_rows, piece, piece_y
    )

    u_far = send(u_over, OUTWARD)
    u_near_over = send(u_near, MIDDLE)
    pieces = jnp.stack([piece, piece_y])
    pieces_c = send(pieces, FLIP_C)
    early = dot_last(jnp.concatenate([g, g_near], axis=0), gate_rows)
    early = early + dot_last(jnp.concatenate([u, u_near], axis=0), up_rows)
    early_keep, early_away = over_core(early[:tokens], early[tokens:])
    g_far, g_near_over, pieces, pieces_c, early_keep, early_away = tie(
        g_far, g_near_over, pieces, pieces_c, early_keep, early_away
    )

    early_recv = send(early_away, FLIP_C)
    g_farthest = send(g_near_over, OUTWARD)
    far = jnp.zeros((3, model_size, piece_rows, plane), bf16)
    for part, place in ((pieces[0], m), (pieces_c[0], m ^ 1), (pieces[1], m ^ 2), (pieces_c[1], m ^ 3)):
        far = lax.dynamic_update_slice(far, part[:, None], (0, place, 0, 0))
    own_inputs = lax.dynamic_slice(layer_input, (0, z * plane), (tokens, plane))
    inputs = jnp.concatenate([own_inputs, far.reshape(3 * tokens, plane)])
    near_tokens = 3 * tokens
    inputs_keep = lax.dynamic_slice(inputs, (0, x * rows), (4 * tokens, rows))
    inputs_away = lax.dynamic_slice(inputs, (0, (1 - x) * rows), (4 * tokens, rows))

    def near_products(block):
        return dot_first(inputs_away[:near_tokens], block), dot_first(inputs_keep[:near_tokens], block)

    def last_products(block, near, span):
        away, keep = near
        away = away[:, span] + dot_first(inputs_away[near_tokens:], block)
        return away.astype(bf16), keep[:, span] + dot_first(inputs_keep[near_tokens:], block)

    g_third = g_near_over + g_far
    g_products = near_products(jnp.concatenate([g, g_near, g_third], axis=0))
    early_keep, early_away = over_y(early_keep + early_recv.astype(f32))
    u_far, u_near_over, g_products, inputs_keep, inputs_away, early_keep, early_away = tie(
        u_far, u_near_over, g_products, inputs_keep, inputs_away, early_keep, early_away
    )

    u_farthest = send(u_near_over, OUTWARD)
    u_third = u_near_over + u_far
    u_products = near_products(jnp.concatenate([u, u_near, u_third], axis=0))
    early_recv = send(early_away, FLIP_Y)
    third = dot_last(g_third, gate_rows) + dot_last(u_third, up_rows)
    u_products, third, early_recv, g_farthest = tie(u_products, third, early_recv, g_farthest)

    g_last = g_over + g_farthest
    away, g_keep = last_products(g_last, g_products, slice(None))
    g_recv = send(away, FLIP_X)
    early_sum = (early_keep + early_recv.astype(f32)).astype(bf16)
    early_home = [send(early_sum, home(0, h)) for h in range(2)]
    g_keep, g_last, u_farthest, g_recv = tie(g_keep, g_last, u_farthest, g_recv)

    block = u_over + u_farthest
    away, up_keep = last_products(block, u_products, slice(None))
    away, block, g_last, early_home = tie(away, block, g_last, early_home)
    up_recv = send(away, FLIP_X)
    last = dot_last(g_last, gate_rows) + dot_last(block, up_rows)
    late_keep, late_away = over_core(third, last)
    late_recv = send(late_away, FLIP_C)
    late_keep, late_away = over_y(late_keep + late_recv.astype(f32))
    gate_gradient = gradient(g_keep, g_recv)
    gate_row = jnp.sum(gate_gradient * gate_gradient, axis=1)
    gate_col = jnp.sum(gate_gradient * gate_gradient, axis=0)
    late_away, late_keep, gate_row, gate_col, gate_gradient, up_keep = tie(
        late_away, late_keep, gate_row, gate_col, gate_gradient, up_keep
    )
    late_recv = send(late_away, FLIP_Y)
    late_sum = (late_keep + late_recv.astype(f32)).astype(bf16)
    late_home = [send(late_sum, home(2, h)) for h in range(2)]
    late_home, up_recv = tie(late_home, up_recv)

    entry_count = rows * data_size * cols * model_size
    up_gradient = gradient(up_keep, up_recv)
    gradients = (gate_gradient, up_gradient)
    squares = up_gradient * up_gradient
    row_total = sum_over(jnp.stack([gate_row, jnp.sum(squares, axis=1)]), OVER_MP)
    new_rows = decay_rate * row_moments + (1.0 - decay_rate) * (row_total / (cols * model_size))
    inverse = 1.0 / new_rows
    column_sums = jnp.concatenate(
        [gate_col, jnp.sum(squares, axis=0)]
        + [jnp.sum(v * v * inverse[k][:, None], axis=0) for k, v in enumerate(gradients)]
    )
    column_sums = sum_over(column_sums, OVER_DP).reshape(2, 2, cols)
    new_cols = decay_rate * col_moments + (1.0 - decay_rate) * (
        column_sums[0] / (rows * data_size)
    )
    square_sums = jnp.sum(column_sums[1] / new_cols, axis=1)
    square_sums = sum_over(jnp.broadcast_to(square_sums[:, None], (2, 128)), OVER_MP)[:, :1]
    row_factor = lax.rsqrt(new_rows) * lax.rsqrt(square_sums / entry_count + 1e-06)
    col_factor = lax.rsqrt(new_cols)
    updates = [
        v * row_factor[k][:, None] * col_factor[k][None, :] for k, v in enumerate(gradients)
    ]
    input_grad = jnp.concatenate([early_home[h] + late_home[h] for h in range(2)], axis=0)
    return input_grad, updates[0], updates[1], new_rows, new_cols


def solution(mesh):
    in_specs = (
        P("dp", None),
        P("dp", "mp"),
        P("dp", "mp"),
        P("dp", "mp"),
        P("dp"),
        P(),
        P("dp", "mp"),
        P("dp", "mp"),
        P(None, "dp"),
        P(None, "mp"),
    )
    out_specs = (P("dp", "mp"), P("dp", "mp"), P("dp", "mp"), P(None, "dp"), P(None, "mp"))
    fits = (mesh.shape["dp"], mesh.shape["mp"]) == (GRID[0] * GRID[1], GRID[2] * GRID[3])
    local = local_block if fits else local_any
    return jax.shard_map(local, mesh=mesh, in_specs=in_specs, out_specs=out_specs, check_vma=False)
```

```python
import functools
import math

import jax
import jax.numpy as jnp
from jax import lax
from jax.experimental import pallas as pl
from jax.experimental.pallas import tpu as pltpu
from jax.sharding import PartitionSpec as P

decay_rate = 0.9
tanh_scale = math.sqrt(2.0 / math.pi)
cubic_term = 0.044715
f32 = jnp.float32
bf16 = jnp.bfloat16
AXES = ("dp", "mp")
GRID = (4, 2, 2, 2)


def gelu_pair(pre_act):
    argument = tanh_scale * (pre_act + cubic_term * pre_act * pre_act * pre_act)
    tangent = jnp.tanh(argument)
    gelu_value = 0.5 * pre_act * (1.0 + tangent)
    gelu_slope = 0.5 * (1.0 + tangent) + 0.5 * pre_act * (1.0 - tangent * tangent) * tanh_scale * (
        1.0 + 3.0 * cubic_term * pre_act * pre_act
    )
    return (gelu_value, gelu_slope)


def token_advantage(teacher_ids, adv_table):
    classes = adv_table.shape[0]
    class_hit = teacher_ids[:, None] == jnp.arange(classes, dtype=jnp.int32)[None, :]
    return jnp.sum(jnp.where(class_hit, adv_table[None, :], 0.0), axis=1)


def local_any(
    layer_input,
    gate_pre,
    up_pre,
    hidden_cot,
    teacher_ids,
    adv_table,
    gate_weight,
    up_weight,
    row_moments,
    col_moments,
):
    data_size = lax.axis_size("dp")
    model_size = lax.axis_size("mp")
    block_rows = gate_weight.shape[0]
    block_cols = gate_weight.shape[1]
    token_count = layer_input.shape[0]
    advantage = token_advantage(teacher_ids, adv_table)
    weighted = hidden_cot.astype(f32) * advantage[:, None]
    gelu_value, gelu_slope = gelu_pair(gate_pre.astype(f32))
    gate_grad = (weighted * up_pre.astype(f32) * gelu_slope).astype(bf16)
    up_grad = (weighted * gelu_value).astype(bf16)
    contract_last = (((1,), (1,)), ((), ()))
    contract_first = (((0,), (0,)), ((), ()))
    pieces = lax.all_gather((gate_weight, up_weight), "dp", axis=0, tiled=True)
    partial_sum = lax.dot_general(
        gate_grad, pieces[0], contract_last, preferred_element_type=f32
    ) + lax.dot_general(up_grad, pieces[1], contract_last, preferred_element_type=f32)
    input_grad = lax.psum_scatter(
        partial_sum.astype(bf16), "mp", scatter_dimension=1, tiled=True
    )
    grad_scale = 1.0 / math.sqrt(token_count * data_size)
    gate_term = lax.dot_general(layer_input, gate_grad, contract_first, preferred_element_type=f32)
    up_term = lax.dot_general(layer_input, up_grad, contract_first, preferred_element_type=f32)
    summed = lax.psum_scatter(
        jnp.concatenate([gate_term, up_term], axis=1).astype(bf16),
        "dp",
        scatter_dimension=0,
        tiled=True,
    ).astype(f32)
    grad_gate = summed[:, :block_cols] * grad_scale
    grad_up = summed[:, block_cols:] * grad_scale
    squares_gate = grad_gate * grad_gate
    squares_up = grad_up * grad_up
    row_local = jnp.stack([jnp.sum(squares_gate, axis=1), jnp.sum(squares_up, axis=1)])
    col_local = jnp.stack([jnp.sum(squares_gate, axis=0), jnp.sum(squares_up, axis=0)])
    row_total = lax.psum(row_local, "mp")
    col_total = lax.psum(col_local, "dp")
    new_rows = decay_rate * row_moments + (1.0 - decay_rate) * (
        row_total / (block_cols * model_size)
    )
    new_cols = decay_rate * col_moments + (1.0 - decay_rate) * (
        col_total / (block_rows * data_size)
    )
    scaled_gate = grad_gate / jnp.sqrt(new_rows[0][:, None] * new_cols[0][None, :])
    scaled_up = grad_up / jnp.sqrt(new_rows[1][:, None] * new_cols[1][None, :])
    square_sums = lax.psum(
        jnp.stack([jnp.sum(scaled_gate * scaled_gate), jnp.sum(scaled_up * scaled_up)]),
        ("dp", "mp"),
    )
    entry_count = block_rows * data_size * block_cols * model_size
    mean_square = square_sums / entry_count
    gate_update = scaled_gate / jnp.sqrt(mean_square[0] + 1e-06)
    up_update = scaled_up / jnp.sqrt(mean_square[1] + 1e-06)
    return (input_grad, gate_update, up_update, new_rows, new_cols)


def device_number(place):
    number = 0
    for coordinate, size in zip(place, GRID):
        number = number * size + coordinate
    return number


def pairs(target):
    out = []
    for z in range(GRID[0]):
        for x in range(GRID[1]):
            for y in range(GRID[2]):
                for c in range(GRID[3]):
                    place = target(z, x, y, c)
                    if place is not None:
                        out.append((device_number((z, x, y, c)), device_number(place)))
    return out


def flip_z(k):
    return pairs(lambda z, x, y, c: (z ^ k, x, y, c))


FLIP_X = pairs(lambda z, x, y, c: (z, 1 - x, y, c))
FLIP_Y = pairs(lambda z, x, y, c: (z, x, 1 - y, c))
FLIP_C = pairs(lambda z, x, y, c: (z, x, y, 1 - c))
MIDDLE = pairs(lambda z, x, y, c: (3 - z, x, y, c) if z in (1, 2) else None)
OUTWARD = pairs(lambda z, x, y, c: ({1: 0, 2: 3}[z], x, y, c) if z in (1, 2) else None)
INWARD = pairs(lambda z, x, y, c: ({0: 1, 3: 2}[z], x, y, c) if z in (0, 3) else None)


def home(first, half):
    return pairs(lambda z, x, y, c: (z ^ (first + c), x, z >> 1, z & 1) if y == half else None)


def home_from(core, k, half):
    return pairs(
        lambda z, x, y, c: (z ^ k, x, z >> 1, z & 1) if (y, c) == (half, core) else None
    )


def to_core(core):
    return pairs(lambda z, x, y, c: (z, x, y, core) if c != core else None)


def flip_y_of(core):
    return pairs(lambda z, x, y, c: (z, x, 1 - y, c) if c == core else None)


def send(value, permutation):
    return lax.ppermute(value, AXES, permutation)


def tie(*values):
    return lax.optimization_barrier(values)


def advantage_of(ids_ref, table_ref):
    ids = ids_ref[...]
    hit = ids == lax.broadcasted_iota(jnp.int32, (ids.shape[0], table_ref.shape[1]), 1)
    return jnp.sum(jnp.where(hit, table_ref[...], 0.0), axis=1, keepdims=True)


def gate_kernel(ids_ref, table_ref, cot_ref, gate_ref, up_ref, out_ref):
    weighted = cot_ref[...].astype(f32) * advantage_of(ids_ref, table_ref)
    slope = gelu_pair(gate_ref[...].astype(f32))[1]
    out_ref[...] = (weighted * up_ref[...].astype(f32) * slope).astype(bf16)


def up_kernel(ids_ref, table_ref, cot_ref, gate_ref, out_ref):
    weighted = cot_ref[...].astype(f32) * advantage_of(ids_ref, table_ref)
    out_ref[...] = (weighted * gelu_pair(gate_ref[...].astype(f32))[0]).astype(bf16)


def front(kernel, teacher_ids, adv_table, arrays):
    tokens, cols = arrays[0].shape
    rows = 128
    block = pl.BlockSpec((rows, cols), lambda i: (i, 0))
    return pl.pallas_call(
        kernel,
        grid=(tokens // rows,),
        in_specs=[
            pl.BlockSpec((rows, 1), lambda i: (i, 0)),
            pl.BlockSpec((1, adv_table.shape[0]), lambda i: (0, 0)),
        ]
        + [block] * len(arrays),
        out_specs=block,
        out_shape=jax.ShapeDtypeStruct((tokens, cols), bf16),
        cost_estimate=pl.CostEstimate(
            flops=tokens * cols, bytes_accessed=tokens * cols, transcendentals=0
        ),
    )(teacher_ids[:, None], adv_table[None, :], *arrays)


def dot_first(a, b):
    return lax.dot_general(a, b, (((0,), (0,)), ((), ())), preferred_element_type=f32)


def dot_last(a, b):
    return lax.dot_general(a, b, (((1,), (1,)), ((), ())), preferred_element_type=f32)


def sum_over(value, permutations):
    for permutation in permutations:
        value = value + send(value, permutation)
    return value


OVER_DP = (FLIP_X, flip_z(1), flip_z(2))
OVER_MP = (FLIP_C, FLIP_Y)


def local_block(
    layer_input,
    gate_pre,
    up_pre,
    hidden_cot,
    teacher_ids,
    adv_table,
    gate_weight,
    up_weight,
    row_moments,
    col_moments,
):
    data_size = lax.axis_size("dp")
    model_size = lax.axis_size("mp")
    rows, cols = gate_weight.shape
    tokens = layer_input.shape[0]
    dp = lax.axis_index("dp")
    m = lax.axis_index("mp")
    z, x = dp // 2, dp % 2
    y, c = m // 2, m % 2
    piece_rows = tokens // model_size
    plane = 2 * rows
    edge = cols * 4 // 10 // 128 * 128
    up_spans = [slice(0, edge), slice(edge, cols)]
    grad_scale = 1.0 / math.sqrt(tokens * data_size)

    def plane_rows(own, other):
        both = jnp.zeros((plane, cols), bf16)
        both = lax.dynamic_update_slice(both, own, (x * rows, 0))
        return lax.dynamic_update_slice(both, other, ((1 - x) * rows, 0))

    def over_core(first, second):
        keep = jnp.where(c == 0, first, second)
        away = jnp.where(c == 0, second, first).astype(bf16)
        return keep, away

    def over_y(block):
        part = tokens // 2
        keep = lax.dynamic_slice(block, (y * part, 0), (part, plane))
        away = lax.dynamic_slice(block, ((1 - y) * part, 0), (part, plane)).astype(bf16)
        return keep, away

    def gradient(keep, recv):
        return (keep + recv.astype(f32)) * grad_scale

    mine = lax.dynamic_slice(layer_input, (m * piece_rows, 0), (piece_rows, layer_input.shape[1]))
    piece = [
        send(lax.dynamic_slice(mine, (0, (z ^ k) * plane), (piece_rows, plane)), flip_z(k))
        for k in (1, 2, 3)
    ]
    gate_other = send(gate_weight, FLIP_X)
    g = front(gate_kernel, teacher_ids, adv_table, (hidden_cot, gate_pre, up_pre))
    u = front(up_kernel, teacher_ids, adv_table, (hidden_cot, gate_pre))
    piece, g, u, gate_other, up_weight = tie(piece, g, u, gate_other, up_weight)

    g_near = send(g, flip_z(1))
    g_over = send(g, MIDDLE)
    u_near = send(u, flip_z(1))
    u_over = send(u, MIDDLE)
    up_other = send(up_weight, FLIP_X)
    piece = jnp.stack(piece)
    g_near, g_over, up_other, piece = tie(g_near, g_over, up_other, piece)

    g_far = send(g_over, OUTWARD)
    g_near_over = send(g_near, MIDDLE)
    piece_y = send(piece, FLIP_Y)
    gate_rows = plane_rows(gate_weight, gate_other)
    up_rows = plane_rows(up_weight, up_other)
    u_near, u_over, gate_rows, up_rows, piece, piece_y = tie(
        u_near, u_over, gate_rows, up_rows, piece, piece_y
    )

    u_near_over = send(u_near, MIDDLE)
    pieces = jnp.stack([piece, piece_y])
    pieces_c = send(pieces, FLIP_C)
    early = dot_last(jnp.concatenate([g, g_near], axis=0), gate_rows)
    early = early + dot_last(jnp.concatenate([u, u_near], axis=0), up_rows)
    early_keep, early_away = over_core(early[:tokens], early[tokens:])
    g_far, g_near_over, pieces, pieces_c, early_keep, early_away, u_over = tie(
        g_far, g_near_over, pieces, pieces_c, early_keep, early_away, u_over
    )

    early_recv = send(early_away, FLIP_C)
    g_farthest = send(g_near_over, OUTWARD)
    u_far = send(u_over, OUTWARD)
    far = jnp.zeros((3, model_size, piece_rows, plane), bf16)
    for part, place in ((pieces[0], m), (pieces_c[0], m ^ 1), (pieces[1], m ^ 2), (pieces_c[1], m ^ 3)):
        far = lax.dynamic_update_slice(far, part[:, None], (0, place, 0, 0))
    own_inputs = lax.dynamic_slice(layer_input, (0, z * plane), (tokens, plane))
    inputs = jnp.concatenate([own_inputs, far.reshape(3 * tokens, plane)])
    near_tokens = 3 * tokens
    inputs_keep = lax.dynamic_slice(inputs, (0, x * rows), (4 * tokens, rows))
    inputs_away = lax.dynamic_slice(inputs, (0, (1 - x) * rows), (4 * tokens, rows))

    def near_products(block):
        return dot_first(inputs_away[:near_tokens], block), dot_first(inputs_keep[:near_tokens], block)

    def last_products(block, near, span):
        away, keep = near
        away = away[:, span] + dot_first(inputs_away[near_tokens:], block)
        return away.astype(bf16), keep[:, span] + dot_first(inputs_keep[near_tokens:], block)

    g_third = g_near_over + g_far
    g_products = near_products(jnp.concatenate([g, g_near, g_third], axis=0))
    early_keep, early_away = over_y(early_keep + early_recv.astype(f32))
    u_near_over, g_farthest, g_products, inputs_keep, inputs_away, early_keep, early_away = tie(
        u_near_over, g_farthest, g_products, inputs_keep, inputs_away, early_keep, early_away
    )

    u_farthest = [send(u_near_over[:, span], OUTWARD) for span in up_spans]
    g_last = g_over + g_farthest
    away, g_keep = last_products(g_last, g_products, slice(None))
    g_recv = send(away, FLIP_X)
    early_recv = send(early_away, FLIP_Y)
    u_far, early_recv, g_keep, g_last = tie(u_far, early_recv, g_keep, g_last)

    u_third = u_near_over + u_far
    u_products = near_products(jnp.concatenate([u, u_near, u_third], axis=0))
    third = dot_last(g_third, gate_rows) + dot_last(u_third, up_rows)
    early_sum = (early_keep + early_recv.astype(f32)).astype(bf16)
    third_recv = send(third.astype(bf16), to_core(0))
    u_products, third, third_recv, early_sum, u_farthest[0], g_recv = tie(
        u_products, third, third_recv, early_sum, u_farthest[0], g_recv
    )

    block = u_over[:, up_spans[0]] + u_farthest[0]
    away, first_keep = last_products(block, u_products, up_spans[0])
    first_recv = send(away, FLIP_X)
    last = dot_last(g_last, gate_rows) + dot_last(block, up_rows[:, up_spans[0]])
    early_home = [send(early_sum, home(0, h)) for h in range(2)]
    third_keep, third_away = over_y(third + third_recv.astype(f32))
    third_recv = send(third_away, flip_y_of(0))
    last, first_keep, first_recv, u_farthest[1], early_home, third_keep, third_recv = tie(
        last, first_keep, first_recv, u_farthest[1], early_home, third_keep, third_recv
    )

    block = u_over[:, up_spans[1]] + u_farthest[1]
    away, second_keep = last_products(block, u_products, up_spans[1])
    second_recv = send(away, FLIP_X)
    last = last + dot_last(block, up_rows[:, up_spans[1]])
    late_recv = send(last.astype(bf16), to_core(1))
    third_sum = (third_keep + third_recv.astype(f32)).astype(bf16)
    third_home = [send(third_sum, home_from(0, 2, h)) for h in range(2)]
    late_keep, late_away = over_y(last + late_recv.astype(f32))
    gate_gradient = gradient(g_keep, g_recv)
    gate_row = jnp.sum(gate_gradient * gate_gradient, axis=1)
    gate_col = jnp.sum(gate_gradient * gate_gradient, axis=0)
    late_away, late_keep, gate_row, gate_col, gate_gradient, second_keep = tie(
        late_away, late_keep, gate_row, gate_col, gate_gradient, second_keep
    )
    late_recv = send(late_away, flip_y_of(1))
    late_recv, second_recv, third_home = tie(late_recv, second_recv, third_home)
    late_sum = (late_keep + late_recv.astype(f32)).astype(bf16)
    late_home = [send(late_sum, home_from(1, 3, h)) for h in range(2)]

    entry_count = rows * data_size * cols * model_size
    up_gradient = jnp.concatenate(
        [gradient(first_keep, first_recv), gradient(second_keep, second_recv)], axis=1
    )
    gradients = (gate_gradient, up_gradient)
    squares = up_gradient * up_gradient
    row_total = sum_over(jnp.stack([gate_row, jnp.sum(squares, axis=1)]), OVER_MP)
    new_rows = decay_rate * row_moments + (1.0 - decay_rate) * (row_total / (cols * model_size))
    inverse = 1.0 / new_rows
    column_sums = jnp.concatenate(
        [gate_col, jnp.sum(squares, axis=0)]
        + [jnp.sum(v * v * inverse[k][:, None], axis=0) for k, v in enumerate(gradients)]
    )
    column_sums = sum_over(column_sums, OVER_DP).reshape(2, 2, cols)
    new_cols = decay_rate * col_moments + (1.0 - decay_rate) * (
        column_sums[0] / (rows * data_size)
    )
    square_sums = jnp.sum(column_sums[1] / new_cols, axis=1)
    square_sums = sum_over(jnp.broadcast_to(square_sums[:, None], (2, 128)), OVER_MP)[:, :1]
    row_factor = lax.rsqrt(new_rows) * lax.rsqrt(square_sums / entry_count + 1e-06)
    col_factor = lax.rsqrt(new_cols)
    updates = [
        v * row_factor[k][:, None] * col_factor[k][None, :] for k, v in enumerate(gradients)
    ]
    input_grad = jnp.concatenate(
        [early_home[h] + third_home[h] + late_home[h] for h in range(2)], axis=0
    )
    return input_grad, updates[0], updates[1], new_rows, new_cols


def solution(mesh):
    in_specs = (
        P("dp", None),
        P("dp", "mp"),
        P("dp", "mp"),
        P("dp", "mp"),
        P("dp"),
        P(),
        P("dp", "mp"),
        P("dp", "mp"),
        P(None, "dp"),
        P(None, "mp"),
    )
    out_specs = (P("dp", "mp"), P("dp", "mp"), P("dp", "mp"), P(None, "dp"), P(None, "mp"))
    fits = (mesh.shape["dp"], mesh.shape["mp"]) == (GRID[0] * GRID[1], GRID[2] * GRID[3])
    local = local_block if fits else local_any
    return jax.shard_map(local, mesh=mesh, in_specs=in_specs, out_specs=out_specs, check_vma=False)
```

```python
import functools
import math

import jax
import jax.numpy as jnp
from jax import lax
from jax.experimental import pallas as pl
from jax.experimental.pallas import tpu as pltpu
from jax.sharding import PartitionSpec as P

decay_rate = 0.9
tanh_scale = math.sqrt(2.0 / math.pi)
cubic_term = 0.044715
f32 = jnp.float32
bf16 = jnp.bfloat16
AXES = ("dp", "mp")
GRID = (4, 2, 2, 2)


def gelu_pair(pre_act):
    argument = tanh_scale * (pre_act + cubic_term * pre_act * pre_act * pre_act)
    tangent = jnp.tanh(argument)
    gelu_value = 0.5 * pre_act * (1.0 + tangent)
    gelu_slope = 0.5 * (1.0 + tangent) + 0.5 * pre_act * (1.0 - tangent * tangent) * tanh_scale * (
        1.0 + 3.0 * cubic_term * pre_act * pre_act
    )
    return (gelu_value, gelu_slope)


def token_advantage(teacher_ids, adv_table):
    classes = adv_table.shape[0]
    class_hit = teacher_ids[:, None] == jnp.arange(classes, dtype=jnp.int32)[None, :]
    return jnp.sum(jnp.where(class_hit, adv_table[None, :], 0.0), axis=1)


def local_any(
    layer_input,
    gate_pre,
    up_pre,
    hidden_cot,
    teacher_ids,
    adv_table,
    gate_weight,
    up_weight,
    row_moments,
    col_moments,
):
    data_size = lax.axis_size("dp")
    model_size = lax.axis_size("mp")
    block_rows = gate_weight.shape[0]
    block_cols = gate_weight.shape[1]
    token_count = layer_input.shape[0]
    advantage = token_advantage(teacher_ids, adv_table)
    weighted = hidden_cot.astype(f32) * advantage[:, None]
    gelu_value, gelu_slope = gelu_pair(gate_pre.astype(f32))
    gate_grad = (weighted * up_pre.astype(f32) * gelu_slope).astype(bf16)
    up_grad = (weighted * gelu_value).astype(bf16)
    contract_last = (((1,), (1,)), ((), ()))
    contract_first = (((0,), (0,)), ((), ()))
    pieces = lax.all_gather((gate_weight, up_weight), "dp", axis=0, tiled=True)
    partial_sum = lax.dot_general(
        gate_grad, pieces[0], contract_last, preferred_element_type=f32
    ) + lax.dot_general(up_grad, pieces[1], contract_last, preferred_element_type=f32)
    input_grad = lax.psum_scatter(
        partial_sum.astype(bf16), "mp", scatter_dimension=1, tiled=True
    )
    grad_scale = 1.0 / math.sqrt(token_count * data_size)
    gate_term = lax.dot_general(layer_input, gate_grad, contract_first, preferred_element_type=f32)
    up_term = lax.dot_general(layer_input, up_grad, contract_first, preferred_element_type=f32)
    summed = lax.psum_scatter(
        jnp.concatenate([gate_term, up_term], axis=1).astype(bf16),
        "dp",
        scatter_dimension=0,
        tiled=True,
    ).astype(f32)
    grad_gate = summed[:, :block_cols] * grad_scale
    grad_up = summed[:, block_cols:] * grad_scale
    squares_gate = grad_gate * grad_gate
    squares_up = grad_up * grad_up
    row_local = jnp.stack([jnp.sum(squares_gate, axis=1), jnp.sum(squares_up, axis=1)])
    col_local = jnp.stack([jnp.sum(squares_gate, axis=0), jnp.sum(squares_up, axis=0)])
    row_total = lax.psum(row_local, "mp")
    col_total = lax.psum(col_local, "dp")
    new_rows = decay_rate * row_moments + (1.0 - decay_rate) * (
        row_total / (block_cols * model_size)
    )
    new_cols = decay_rate * col_moments + (1.0 - decay_rate) * (
        col_total / (block_rows * data_size)
    )
    scaled_gate = grad_gate / jnp.sqrt(new_rows[0][:, None] * new_cols[0][None, :])
    scaled_up = grad_up / jnp.sqrt(new_rows[1][:, None] * new_cols[1][None, :])
    square_sums = lax.psum(
        jnp.stack([jnp.sum(scaled_gate * scaled_gate), jnp.sum(scaled_up * scaled_up)]),
        ("dp", "mp"),
    )
    entry_count = block_rows * data_size * block_cols * model_size
    mean_square = square_sums / entry_count
    gate_update = scaled_gate / jnp.sqrt(mean_square[0] + 1e-06)
    up_update = scaled_up / jnp.sqrt(mean_square[1] + 1e-06)
    return (input_grad, gate_update, up_update, new_rows, new_cols)


def device_number(place):
    number = 0
    for coordinate, size in zip(place, GRID):
        number = number * size + coordinate
    return number


def pairs(target):
    out = []
    for z in range(GRID[0]):
        for x in range(GRID[1]):
            for y in range(GRID[2]):
                for c in range(GRID[3]):
                    place = target(z, x, y, c)
                    if place is not None:
                        out.append((device_number((z, x, y, c)), device_number(place)))
    return out


def flip_z(k):
    return pairs(lambda z, x, y, c: (z ^ k, x, y, c))


FLIP_X = pairs(lambda z, x, y, c: (z, 1 - x, y, c))
FLIP_Y = pairs(lambda z, x, y, c: (z, x, 1 - y, c))
FLIP_C = pairs(lambda z, x, y, c: (z, x, y, 1 - c))
MIDDLE = pairs(lambda z, x, y, c: (3 - z, x, y, c) if z in (1, 2) else None)
OUTWARD = pairs(lambda z, x, y, c: ({1: 0, 2: 3}[z], x, y, c) if z in (1, 2) else None)
INWARD = pairs(lambda z, x, y, c: ({0: 1, 3: 2}[z], x, y, c) if z in (0, 3) else None)


def home(first, half):
    return pairs(lambda z, x, y, c: (z ^ (first + c), x, z >> 1, z & 1) if y == half else None)


def home_from(core, k, half):
    return pairs(
        lambda z, x, y, c: (z ^ k, x, z >> 1, z & 1) if (y, c) == (half, core) else None
    )


def to_core(core):
    return pairs(lambda z, x, y, c: (z, x, y, core) if c != core else None)


def flip_y_of(core):
    return pairs(lambda z, x, y, c: (z, x, 1 - y, c) if c == core else None)


def send(value, permutation):
    return lax.ppermute(value, AXES, permutation)


def tie(*values):
    return lax.optimization_barrier(values)


def advantage_of(ids_ref, table_ref):
    ids = ids_ref[...]
    hit = ids == lax.broadcasted_iota(jnp.int32, (ids.shape[0], table_ref.shape[1]), 1)
    return jnp.sum(jnp.where(hit, table_ref[...], 0.0), axis=1, keepdims=True)


def gate_kernel(ids_ref, table_ref, cot_ref, gate_ref, up_ref, out_ref):
    weighted = cot_ref[...].astype(f32) * advantage_of(ids_ref, table_ref)
    slope = gelu_pair(gate_ref[...].astype(f32))[1]
    out_ref[...] = (weighted * up_ref[...].astype(f32) * slope).astype(bf16)


def up_kernel(ids_ref, table_ref, cot_ref, gate_ref, out_ref):
    weighted = cot_ref[...].astype(f32) * advantage_of(ids_ref, table_ref)
    out_ref[...] = (weighted * gelu_pair(gate_ref[...].astype(f32))[0]).astype(bf16)


def front(kernel, teacher_ids, adv_table, arrays):
    tokens, cols = arrays[0].shape
    rows = 128
    block = pl.BlockSpec((rows, cols), lambda i: (i, 0))
    return pl.pallas_call(
        kernel,
        grid=(tokens // rows,),
        in_specs=[
            pl.BlockSpec((rows, 1), lambda i: (i, 0)),
            pl.BlockSpec((1, adv_table.shape[0]), lambda i: (0, 0)),
        ]
        + [block] * len(arrays),
        out_specs=block,
        out_shape=jax.ShapeDtypeStruct((tokens, cols), bf16),
        cost_estimate=pl.CostEstimate(
            flops=tokens * cols, bytes_accessed=tokens * cols, transcendentals=0
        ),
    )(teacher_ids[:, None], adv_table[None, :], *arrays)


def dot_first(a, b):
    return lax.dot_general(a, b, (((0,), (0,)), ((), ())), preferred_element_type=f32)


def dot_last(a, b):
    return lax.dot_general(a, b, (((1,), (1,)), ((), ())), preferred_element_type=f32)


def sum_over(value, permutations):
    for permutation in permutations:
        value = value + send(value, permutation)
    return value


OVER_DP = (FLIP_X, flip_z(1), flip_z(2))
OVER_MP = (FLIP_C, FLIP_Y)


def local_block(
    layer_input,
    gate_pre,
    up_pre,
    hidden_cot,
    teacher_ids,
    adv_table,
    gate_weight,
    up_weight,
    row_moments,
    col_moments,
):
    data_size = lax.axis_size("dp")
    model_size = lax.axis_size("mp")
    rows, cols = gate_weight.shape
    tokens = layer_input.shape[0]
    dp = lax.axis_index("dp")
    m = lax.axis_index("mp")
    z, x = dp // 2, dp % 2
    y, c = m // 2, m % 2
    piece_rows = tokens // model_size
    plane = 2 * rows
    edge = cols * 4 // 10 // 128 * 128
    up_spans = [slice(0, edge), slice(edge, cols)]
    grad_scale = 1.0 / math.sqrt(tokens * data_size)

    def plane_rows(own, other):
        both = jnp.zeros((plane, cols), bf16)
        both = lax.dynamic_update_slice(both, own, (x * rows, 0))
        return lax.dynamic_update_slice(both, other, ((1 - x) * rows, 0))

    def over_core(first, second):
        keep = jnp.where(c == 0, first, second)
        away = jnp.where(c == 0, second, first).astype(bf16)
        return keep, away

    def over_y(block):
        part = tokens // 2
        keep = lax.dynamic_slice(block, (y * part, 0), (part, plane))
        away = lax.dynamic_slice(block, ((1 - y) * part, 0), (part, plane)).astype(bf16)
        return keep, away

    def gradient(keep, recv):
        return (keep + recv.astype(f32)) * grad_scale

    mine = lax.dynamic_slice(layer_input, (m * piece_rows, 0), (piece_rows, layer_input.shape[1]))
    piece = [
        send(lax.dynamic_slice(mine, (0, (z ^ k) * plane), (piece_rows, plane)), flip_z(k))
        for k in (1, 2, 3)
    ]
    gate_other = send(gate_weight, FLIP_X)
    g = front(gate_kernel, teacher_ids, adv_table, (hidden_cot, gate_pre, up_pre))
    u = front(up_kernel, teacher_ids, adv_table, (hidden_cot, gate_pre))
    piece, g, u, gate_other, up_weight = tie(piece, g, u, gate_other, up_weight)

    g_near = send(g, flip_z(1))
    g_over = send(g, MIDDLE)
    u_near = send(u, flip_z(1))
    u_over = send(u, MIDDLE)
    up_other = send(up_weight, FLIP_X)
    piece = jnp.stack(piece)
    g_near, g_over, up_other, piece = tie(g_near, g_over, up_other, piece)

    g_far = send(g_over, OUTWARD)
    g_near_over = send(g_near, MIDDLE)
    piece_y = send(piece, FLIP_Y)
    gate_rows = plane_rows(gate_weight, gate_other)
    up_rows = plane_rows(up_weight, up_other)
    u_near, u_over, gate_rows, up_rows, piece, piece_y = tie(
        u_near, u_over, gate_rows, up_rows, piece, piece_y
    )

    u_near_over = send(u_near, MIDDLE)
    pieces = jnp.stack([piece, piece_y])
    pieces_c = send(pieces, FLIP_C)
    early = dot_last(jnp.concatenate([g, g_near], axis=0), gate_rows)
    early = early + dot_last(jnp.concatenate([u, u_near], axis=0), up_rows)
    early_keep, early_away = over_core(early[:tokens], early[tokens:])
    early_recv = send(early_away, FLIP_C)
    g_far, g_near_over, pieces, pieces_c, early_keep, early_recv, u_over = tie(
        g_far, g_near_over, pieces, pieces_c, early_keep, early_recv, u_over
    )

    early_keep, early_away = over_y(early_keep + early_recv.astype(f32))
    early_recv = send(early_away, FLIP_Y)
    g_farthest = send(g_near_over, OUTWARD)
    u_far = send(u_over, OUTWARD)
    far = jnp.zeros((3, model_size, piece_rows, plane), bf16)
    for part, place in ((pieces[0], m), (pieces_c[0], m ^ 1), (pieces[1], m ^ 2), (pieces_c[1], m ^ 3)):
        far = lax.dynamic_update_slice(far, part[:, None], (0, place, 0, 0))
    own_inputs = lax.dynamic_slice(layer_input, (0, z * plane), (tokens, plane))
    inputs = jnp.concatenate([own_inputs, far.reshape(3 * tokens, plane)])
    near_tokens = 3 * tokens
    inputs_keep = lax.dynamic_slice(inputs, (0, x * rows), (4 * tokens, rows))
    inputs_away = lax.dynamic_slice(inputs, (0, (1 - x) * rows), (4 * tokens, rows))

    def near_products(block):
        return dot_first(inputs_away[:near_tokens], block), dot_first(inputs_keep[:near_tokens], block)

    def last_products(block, near, span):
        away, keep = near
        away = away[:, span] + dot_first(inputs_away[near_tokens:], block)
        return away.astype(bf16), keep[:, span] + dot_first(inputs_keep[near_tokens:], block)

    g_third = g_near_over + g_far
    g_products = near_products(jnp.concatenate([g, g_near, g_third], axis=0))
    early_sum = (early_keep + early_recv.astype(f32)).astype(bf16)
    u_near_over, g_farthest, g_products, inputs_keep, inputs_away, early_sum = tie(
        u_near_over, g_farthest, g_products, inputs_keep, inputs_away, early_sum
    )

    u_farthest = [send(u_near_over[:, up_spans[0]], OUTWARD)]
    g_last = g_over + g_farthest
    away, g_keep = last_products(g_last, g_products, slice(None))
    g_recv = send(away, FLIP_X)
    early_home = [send(early_sum, home(0, h)) for h in range(2)]
    u_far, early_home, g_keep, g_last, u_near_over = tie(u_far, early_home, g_keep, g_last, u_near_over)

    u_farthest.append(send(u_near_over[:, up_spans[1]], OUTWARD))
    u_third = u_near_over + u_far
    u_products = near_products(jnp.concatenate([u, u_near, u_third], axis=0))
    third = dot_last(g_third, gate_rows) + dot_last(u_third, up_rows)
    third_recv = send(third.astype(bf16), to_core(0))
    u_products, third, third_recv, u_farthest[0], g_recv = tie(
        u_products, third, third_recv, u_farthest[0], g_recv
    )

    block = u_over[:, up_spans[0]] + u_farthest[0]
    away, first_keep = last_products(block, u_products, up_spans[0])
    first_recv = send(away, FLIP_X)
    last = dot_last(g_last, gate_rows) + dot_last(block, up_rows[:, up_spans[0]])
    third_keep, third_away = over_y(third + third_recv.astype(f32))
    third_recv = send(third_away, flip_y_of(0))
    last, first_keep, first_recv, u_farthest[1], third_keep, third_recv = tie(
        last, first_keep, first_recv, u_farthest[1], third_keep, third_recv
    )

    block = u_over[:, up_spans[1]] + u_farthest[1]
    away, second_keep = last_products(block, u_products, up_spans[1])
    second_recv = send(away, FLIP_X)
    last = last + dot_last(block, up_rows[:, up_spans[1]])
    late_recv = send(last.astype(bf16), to_core(1))
    third_sum = (third_keep + third_recv.astype(f32)).astype(bf16)
    third_home = [send(third_sum, home_from(0, 2, h)) for h in range(2)]
    late_keep, late_away = over_y(last + late_recv.astype(f32))
    gate_gradient = gradient(g_keep, g_recv)
    gate_row = jnp.sum(gate_gradient * gate_gradient, axis=1)
    gate_col = jnp.sum(gate_gradient * gate_gradient, axis=0)
    late_away, late_keep, gate_row, gate_col, gate_gradient, second_keep = tie(
        late_away, late_keep, gate_row, gate_col, gate_gradient, second_keep
    )
    late_recv = send(late_away, flip_y_of(1))
    late_recv, second_recv, third_home = tie(late_recv, second_recv, third_home)
    late_sum = (late_keep + late_recv.astype(f32)).astype(bf16)
    late_home = [send(late_sum, home_from(1, 3, h)) for h in range(2)]

    entry_count = rows * data_size * cols * model_size
    up_gradient = jnp.concatenate(
        [gradient(first_keep, first_recv), gradient(second_keep, second_recv)], axis=1
    )
    gradients = (gate_gradient, up_gradient)
    squares = up_gradient * up_gradient
    row_total = sum_over(jnp.stack([gate_row, jnp.sum(squares, axis=1)]), OVER_MP)
    new_rows = decay_rate * row_moments + (1.0 - decay_rate) * (row_total / (cols * model_size))
    inverse = 1.0 / new_rows
    column_sums = jnp.concatenate(
        [gate_col, jnp.sum(squares, axis=0)]
        + [jnp.sum(v * v * inverse[k][:, None], axis=0) for k, v in enumerate(gradients)]
    )
    column_sums = sum_over(column_sums, OVER_DP).reshape(2, 2, cols)
    new_cols = decay_rate * col_moments + (1.0 - decay_rate) * (
        column_sums[0] / (rows * data_size)
    )
    square_sums = jnp.sum(column_sums[1] / new_cols, axis=1)
    square_sums = sum_over(jnp.broadcast_to(square_sums[:, None], (2, 128)), OVER_MP)[:, :1]
    row_factor = lax.rsqrt(new_rows) * lax.rsqrt(square_sums / entry_count + 1e-06)
    col_factor = lax.rsqrt(new_cols)
    updates = [
        v * row_factor[k][:, None] * col_factor[k][None, :] for k, v in enumerate(gradients)
    ]
    input_grad = jnp.concatenate(
        [early_home[h] + third_home[h] + late_home[h] for h in range(2)], axis=0
    )
    return input_grad, updates[0], updates[1], new_rows, new_cols


def solution(mesh):
    in_specs = (
        P("dp", None),
        P("dp", "mp"),
        P("dp", "mp"),
        P("dp", "mp"),
        P("dp"),
        P(),
        P("dp", "mp"),
        P("dp", "mp"),
        P(None, "dp"),
        P(None, "mp"),
    )
    out_specs = (P("dp", "mp"), P("dp", "mp"), P("dp", "mp"), P(None, "dp"), P(None, "mp"))
    fits = (mesh.shape["dp"], mesh.shape["mp"]) == (GRID[0] * GRID[1], GRID[2] * GRID[3])
    local = local_block if fits else local_any
    return jax.shard_map(local, mesh=mesh, in_specs=in_specs, out_specs=out_specs, check_vma=False)
```

```python
import functools
import math

import jax
import jax.numpy as jnp
from jax import lax
from jax.experimental import pallas as pl
from jax.experimental.pallas import tpu as pltpu
from jax.sharding import PartitionSpec as P

decay_rate = 0.9
tanh_scale = math.sqrt(2.0 / math.pi)
cubic_term = 0.044715
f32 = jnp.float32
bf16 = jnp.bfloat16
AXES = ("dp", "mp")
GRID = (4, 2, 2, 2)


def gelu_pair(pre_act):
    argument = tanh_scale * (pre_act + cubic_term * pre_act * pre_act * pre_act)
    tangent = jnp.tanh(argument)
    gelu_value = 0.5 * pre_act * (1.0 + tangent)
    gelu_slope = 0.5 * (1.0 + tangent) + 0.5 * pre_act * (1.0 - tangent * tangent) * tanh_scale * (
        1.0 + 3.0 * cubic_term * pre_act * pre_act
    )
    return (gelu_value, gelu_slope)


def token_advantage(teacher_ids, adv_table):
    classes = adv_table.shape[0]
    class_hit = teacher_ids[:, None] == jnp.arange(classes, dtype=jnp.int32)[None, :]
    return jnp.sum(jnp.where(class_hit, adv_table[None, :], 0.0), axis=1)


def local_any(
    layer_input,
    gate_pre,
    up_pre,
    hidden_cot,
    teacher_ids,
    adv_table,
    gate_weight,
    up_weight,
    row_moments,
    col_moments,
):
    data_size = lax.axis_size("dp")
    model_size = lax.axis_size("mp")
    block_rows = gate_weight.shape[0]
    block_cols = gate_weight.shape[1]
    token_count = layer_input.shape[0]
    advantage = token_advantage(teacher_ids, adv_table)
    weighted = hidden_cot.astype(f32) * advantage[:, None]
    gelu_value, gelu_slope = gelu_pair(gate_pre.astype(f32))
    gate_grad = (weighted * up_pre.astype(f32) * gelu_slope).astype(bf16)
    up_grad = (weighted * gelu_value).astype(bf16)
    contract_last = (((1,), (1,)), ((), ()))
    contract_first = (((0,), (0,)), ((), ()))
    pieces = lax.all_gather((gate_weight, up_weight), "dp", axis=0, tiled=True)
    partial_sum = lax.dot_general(
        gate_grad, pieces[0], contract_last, preferred_element_type=f32
    ) + lax.dot_general(up_grad, pieces[1], contract_last, preferred_element_type=f32)
    input_grad = lax.psum_scatter(
        partial_sum.astype(bf16), "mp", scatter_dimension=1, tiled=True
    )
    grad_scale = 1.0 / math.sqrt(token_count * data_size)
    gate_term = lax.dot_general(layer_input, gate_grad, contract_first, preferred_element_type=f32)
    up_term = lax.dot_general(layer_input, up_grad, contract_first, preferred_element_type=f32)
    summed = lax.psum_scatter(
        jnp.concatenate([gate_term, up_term], axis=1).astype(bf16),
        "dp",
        scatter_dimension=0,
        tiled=True,
    ).astype(f32)
    grad_gate = summed[:, :block_cols] * grad_scale
    grad_up = summed[:, block_cols:] * grad_scale
    squares_gate = grad_gate * grad_gate
    squares_up = grad_up * grad_up
    row_local = jnp.stack([jnp.sum(squares_gate, axis=1), jnp.sum(squares_up, axis=1)])
    col_local = jnp.stack([jnp.sum(squares_gate, axis=0), jnp.sum(squares_up, axis=0)])
    row_total = lax.psum(row_local, "mp")
    col_total = lax.psum(col_local, "dp")
    new_rows = decay_rate * row_moments + (1.0 - decay_rate) * (
        row_total / (block_cols * model_size)
    )
    new_cols = decay_rate * col_moments + (1.0 - decay_rate) * (
        col_total / (block_rows * data_size)
    )
    scaled_gate = grad_gate / jnp.sqrt(new_rows[0][:, None] * new_cols[0][None, :])
    scaled_up = grad_up / jnp.sqrt(new_rows[1][:, None] * new_cols[1][None, :])
    square_sums = lax.psum(
        jnp.stack([jnp.sum(scaled_gate * scaled_gate), jnp.sum(scaled_up * scaled_up)]),
        ("dp", "mp"),
    )
    entry_count = block_rows * data_size * block_cols * model_size
    mean_square = square_sums / entry_count
    gate_update = scaled_gate / jnp.sqrt(mean_square[0] + 1e-06)
    up_update = scaled_up / jnp.sqrt(mean_square[1] + 1e-06)
    return (input_grad, gate_update, up_update, new_rows, new_cols)


def device_number(place):
    number = 0
    for coordinate, size in zip(place, GRID):
        number = number * size + coordinate
    return number


def pairs(target):
    out = []
    for z in range(GRID[0]):
        for x in range(GRID[1]):
            for y in range(GRID[2]):
                for c in range(GRID[3]):
                    place = target(z, x, y, c)
                    if place is not None:
                        out.append((device_number((z, x, y, c)), device_number(place)))
    return out


def flip_z(k):
    return pairs(lambda z, x, y, c: (z ^ k, x, y, c))


FLIP_X = pairs(lambda z, x, y, c: (z, 1 - x, y, c))
FLIP_Y = pairs(lambda z, x, y, c: (z, x, 1 - y, c))
FLIP_C = pairs(lambda z, x, y, c: (z, x, y, 1 - c))
MIDDLE = pairs(lambda z, x, y, c: (3 - z, x, y, c) if z in (1, 2) else None)
OUTWARD = pairs(lambda z, x, y, c: ({1: 0, 2: 3}[z], x, y, c) if z in (1, 2) else None)
INWARD = pairs(lambda z, x, y, c: ({0: 1, 3: 2}[z], x, y, c) if z in (0, 3) else None)


def home(first, half):
    return pairs(lambda z, x, y, c: (z ^ (first + c), x, z >> 1, z & 1) if y == half else None)


def home_from(core, k, half):
    return pairs(
        lambda z, x, y, c: (z ^ k, x, z >> 1, z & 1) if (y, c) == (half, core) else None
    )


def to_core(core):
    return pairs(lambda z, x, y, c: (z, x, y, core) if c != core else None)


def flip_y_of(core):
    return pairs(lambda z, x, y, c: (z, x, 1 - y, c) if c == core else None)


def send(value, permutation):
    return lax.ppermute(value, AXES, permutation)


def tie(*values):
    return lax.optimization_barrier(values)


def advantage_of(ids_ref, table_ref):
    ids = ids_ref[...]
    hit = ids == lax.broadcasted_iota(jnp.int32, (ids.shape[0], table_ref.shape[1]), 1)
    return jnp.sum(jnp.where(hit, table_ref[...], 0.0), axis=1, keepdims=True)


def gate_kernel(ids_ref, table_ref, cot_ref, gate_ref, up_ref, out_ref):
    weighted = cot_ref[...].astype(f32) * advantage_of(ids_ref, table_ref)
    slope = gelu_pair(gate_ref[...].astype(f32))[1]
    out_ref[...] = (weighted * up_ref[...].astype(f32) * slope).astype(bf16)


def up_kernel(ids_ref, table_ref, cot_ref, gate_ref, out_ref):
    weighted = cot_ref[...].astype(f32) * advantage_of(ids_ref, table_ref)
    out_ref[...] = (weighted * gelu_pair(gate_ref[...].astype(f32))[0]).astype(bf16)


def front(kernel, teacher_ids, adv_table, arrays):
    tokens, cols = arrays[0].shape
    rows = 128
    block = pl.BlockSpec((rows, cols), lambda i: (i, 0))
    return pl.pallas_call(
        kernel,
        grid=(tokens // rows,),
        in_specs=[
            pl.BlockSpec((rows, 1), lambda i: (i, 0)),
            pl.BlockSpec((1, adv_table.shape[0]), lambda i: (0, 0)),
        ]
        + [block] * len(arrays),
        out_specs=block,
        out_shape=jax.ShapeDtypeStruct((tokens, cols), bf16),
        cost_estimate=pl.CostEstimate(
            flops=tokens * cols, bytes_accessed=tokens * cols, transcendentals=0
        ),
    )(teacher_ids[:, None], adv_table[None, :], *arrays)


def dot_first(a, b):
    return lax.dot_general(a, b, (((0,), (0,)), ((), ())), preferred_element_type=f32)


def dot_last(a, b):
    return lax.dot_general(a, b, (((1,), (1,)), ((), ())), preferred_element_type=f32)


def sum_over(value, permutations):
    for permutation in permutations:
        value = value + send(value, permutation)
    return value


OVER_DP = (FLIP_X, flip_z(1), flip_z(2))
OVER_MP = (FLIP_C, FLIP_Y)


def local_block(
    layer_input,
    gate_pre,
    up_pre,
    hidden_cot,
    teacher_ids,
    adv_table,
    gate_weight,
    up_weight,
    row_moments,
    col_moments,
):
    data_size = lax.axis_size("dp")
    model_size = lax.axis_size("mp")
    rows, cols = gate_weight.shape
    tokens = layer_input.shape[0]
    dp = lax.axis_index("dp")
    m = lax.axis_index("mp")
    z, x = dp // 2, dp % 2
    y, c = m // 2, m % 2
    piece_rows = tokens // model_size
    plane = 2 * rows
    edge = cols * 4 // 10 // 128 * 128
    up_spans = [slice(0, edge), slice(edge, cols)]
    grad_scale = 1.0 / math.sqrt(tokens * data_size)

    def plane_rows(own, other):
        both = jnp.zeros((plane, cols), bf16)
        both = lax.dynamic_update_slice(both, own, (x * rows, 0))
        return lax.dynamic_update_slice(both, other, ((1 - x) * rows, 0))

    def over_core(first, second):
        keep = jnp.where(c == 0, first, second)
        away = jnp.where(c == 0, second, first).astype(bf16)
        return keep, away

    def over_y(block):
        part = tokens // 2
        keep = lax.dynamic_slice(block, (y * part, 0), (part, plane))
        away = lax.dynamic_slice(block, ((1 - y) * part, 0), (part, plane)).astype(bf16)
        return keep, away

    def gradient(keep, recv):
        return (keep + recv.astype(f32)) * grad_scale

    mine = lax.dynamic_slice(layer_input, (m * piece_rows, 0), (piece_rows, layer_input.shape[1]))
    piece = [
        send(lax.dynamic_slice(mine, (0, (z ^ k) * plane), (piece_rows, plane)), flip_z(k))
        for k in (1, 2, 3)
    ]
    g = front(gate_kernel, teacher_ids, adv_table, (hidden_cot, gate_pre, up_pre))
    u = front(up_kernel, teacher_ids, adv_table, (hidden_cot, gate_pre))
    piece, g, u, gate_weight, up_weight = tie(piece, g, u, gate_weight, up_weight)
    gate_other = send(gate_weight, FLIP_X)

    g_near = send(g, flip_z(1))
    g_over = send(g, MIDDLE)
    u_near = send(u, flip_z(1))
    u_over = send(u, MIDDLE)
    piece = jnp.stack(piece)
    g_near, g_over, gate_other, piece, up_weight = tie(g_near, g_over, gate_other, piece, up_weight)
    up_other = send(up_weight, FLIP_X)

    g_far = send(g_over, OUTWARD)
    g_near_over = send(g_near, MIDDLE)
    piece_y = send(piece, FLIP_Y)
    gate_rows = plane_rows(gate_weight, gate_other)
    u_near, u_over, gate_rows, up_other, piece, piece_y = tie(
        u_near, u_over, gate_rows, up_other, piece, piece_y
    )
    up_rows = plane_rows(up_weight, up_other)

    u_near_over = send(u_near, MIDDLE)
    pieces = jnp.stack([piece, piece_y])
    pieces_c = send(pieces, FLIP_C)
    early = dot_last(jnp.concatenate([g, g_near], axis=0), gate_rows)
    early = early + dot_last(jnp.concatenate([u, u_near], axis=0), up_rows)
    early_keep, early_away = over_core(early[:tokens], early[tokens:])
    early_recv = send(early_away, FLIP_C)
    g_far, g_near_over, pieces, pieces_c, early_keep, early_recv, u_over = tie(
        g_far, g_near_over, pieces, pieces_c, early_keep, early_recv, u_over
    )

    early_sum = early_keep + early_recv.astype(f32)
    g_farthest = send(g_near_over, OUTWARD)
    early_keep, early_away = over_y(early_sum)
    early_recv = send(early_away, FLIP_Y)
    u_far = send(u_over, OUTWARD)
    far = jnp.zeros((3, model_size, piece_rows, plane), bf16)
    for part, place in ((pieces[0], m), (pieces_c[0], m ^ 1), (pieces[1], m ^ 2), (pieces_c[1], m ^ 3)):
        far = lax.dynamic_update_slice(far, part[:, None], (0, place, 0, 0))
    own_inputs = lax.dynamic_slice(layer_input, (0, z * plane), (tokens, plane))
    inputs = jnp.concatenate([own_inputs, far.reshape(3 * tokens, plane)])
    near_tokens = 3 * tokens
    inputs_keep = lax.dynamic_slice(inputs, (0, x * rows), (4 * tokens, rows))
    inputs_away = lax.dynamic_slice(inputs, (0, (1 - x) * rows), (4 * tokens, rows))

    def near_products(block):
        return dot_first(inputs_away[:near_tokens], block), dot_first(inputs_keep[:near_tokens], block)

    def last_products(block, near, span):
        away, keep = near
        away = away[:, span] + dot_first(inputs_away[near_tokens:], block)
        return away.astype(bf16), keep[:, span] + dot_first(inputs_keep[near_tokens:], block)

    g_third = g_near_over + g_far
    g_products = near_products(jnp.concatenate([g, g_near, g_third], axis=0))
    early_sum = (early_keep + early_recv.astype(f32)).astype(bf16)
    u_near_over, g_farthest, g_products, inputs_keep, inputs_away, early_sum = tie(
        u_near_over, g_farthest, g_products, inputs_keep, inputs_away, early_sum
    )

    u_farthest = [send(u_near_over[:, up_spans[0]], OUTWARD)]
    g_last = g_over + g_farthest
    away, g_keep = last_products(g_last, g_products, slice(None))
    g_recv = send(away, FLIP_X)
    early_home = [send(early_sum, home(0, h)) for h in range(2)]
    u_far, early_home, g_keep, g_last, u_near_over = tie(u_far, early_home, g_keep, g_last, u_near_over)

    u_farthest.append(send(u_near_over[:, up_spans[1]], OUTWARD))
    u_third = u_near_over + u_far
    u_products = near_products(jnp.concatenate([u, u_near, u_third], axis=0))
    third = dot_last(g_third, gate_rows) + dot_last(u_third, up_rows)
    third_recv = send(third.astype(bf16), to_core(0))
    u_products, third, third_recv, u_farthest[0], g_recv = tie(
        u_products, third, third_recv, u_farthest[0], g_recv
    )

    block = u_over[:, up_spans[0]] + u_farthest[0]
    away, first_keep = last_products(block, u_products, up_spans[0])
    first_recv = send(away, FLIP_X)
    last = dot_last(g_last, gate_rows) + dot_last(block, up_rows[:, up_spans[0]])
    third_keep, third_away = over_y(third + third_recv.astype(f32))
    third_recv = send(third_away, flip_y_of(0))
    last, first_keep, first_recv, u_farthest[1], third_keep, third_recv = tie(
        last, first_keep, first_recv, u_farthest[1], third_keep, third_recv
    )

    block = u_over[:, up_spans[1]] + u_farthest[1]
    away, second_keep = last_products(block, u_products, up_spans[1])
    second_recv = send(away, FLIP_X)
    last = last + dot_last(block, up_rows[:, up_spans[1]])
    late_recv = send(last.astype(bf16), to_core(1))
    third_sum = (third_keep + third_recv.astype(f32)).astype(bf16)
    third_home = [send(third_sum, home_from(0, 2, h)) for h in range(2)]
    late_keep, late_away = over_y(last + late_recv.astype(f32))
    gate_gradient = gradient(g_keep, g_recv)
    gate_row = jnp.sum(gate_gradient * gate_gradient, axis=1)
    gate_col = jnp.sum(gate_gradient * gate_gradient, axis=0)
    late_away, late_keep, gate_row, gate_col, gate_gradient, second_keep = tie(
        late_away, late_keep, gate_row, gate_col, gate_gradient, second_keep
    )
    late_recv = send(late_away, flip_y_of(1))
    late_recv, second_recv, third_home = tie(late_recv, second_recv, third_home)
    late_sum = (late_keep + late_recv.astype(f32)).astype(bf16)
    late_home = [send(late_sum, home_from(1, 3, h)) for h in range(2)]

    entry_count = rows * data_size * cols * model_size
    up_gradient = jnp.concatenate(
        [gradient(first_keep, first_recv), gradient(second_keep, second_recv)], axis=1
    )
    gradients = (gate_gradient, up_gradient)
    squares = up_gradient * up_gradient
    row_total = sum_over(jnp.stack([gate_row, jnp.sum(squares, axis=1)]), OVER_MP)
    new_rows = decay_rate * row_moments + (1.0 - decay_rate) * (row_total / (cols * model_size))
    inverse = 1.0 / new_rows
    column_sums = jnp.concatenate(
        [gate_col, jnp.sum(squares, axis=0)]
        + [jnp.sum(v * v * inverse[k][:, None], axis=0) for k, v in enumerate(gradients)]
    )
    column_sums = sum_over(column_sums, OVER_DP).reshape(2, 2, cols)
    new_cols = decay_rate * col_moments + (1.0 - decay_rate) * (
        column_sums[0] / (rows * data_size)
    )
    square_sums = jnp.sum(column_sums[1] / new_cols, axis=1)
    square_sums = sum_over(jnp.broadcast_to(square_sums[:, None], (2, 128)), OVER_MP)[:, :1]
    row_factor = lax.rsqrt(new_rows) * lax.rsqrt(square_sums / entry_count + 1e-06)
    col_factor = lax.rsqrt(new_cols)
    updates = [
        v * row_factor[k][:, None] * col_factor[k][None, :] for k, v in enumerate(gradients)
    ]
    input_grad = jnp.concatenate(
        [early_home[h] + third_home[h] + late_home[h] for h in range(2)], axis=0
    )
    return input_grad, updates[0], updates[1], new_rows, new_cols


def solution(mesh):
    in_specs = (
        P("dp", None),
        P("dp", "mp"),
        P("dp", "mp"),
        P("dp", "mp"),
        P("dp"),
        P(),
        P("dp", "mp"),
        P("dp", "mp"),
        P(None, "dp"),
        P(None, "mp"),
    )
    out_specs = (P("dp", "mp"), P("dp", "mp"), P("dp", "mp"), P(None, "dp"), P(None, "mp"))
    fits = (mesh.shape["dp"], mesh.shape["mp"]) == (GRID[0] * GRID[1], GRID[2] * GRID[3])
    local = local_block if fits else local_any
    return jax.shard_map(local, mesh=mesh, in_specs=in_specs, out_specs=out_specs, check_vma=False)
```

```python
import functools
import math

import jax
import jax.numpy as jnp
from jax import lax
from jax.experimental import pallas as pl
from jax.experimental.pallas import tpu as pltpu
from jax.sharding import PartitionSpec as P

decay_rate = 0.9
tanh_scale = math.sqrt(2.0 / math.pi)
cubic_term = 0.044715
f32 = jnp.float32
bf16 = jnp.bfloat16
AXES = ("dp", "mp")
GRID = (4, 2, 2, 2)


def gelu_pair(pre_act):
    argument = tanh_scale * (pre_act + cubic_term * pre_act * pre_act * pre_act)
    tangent = jnp.tanh(argument)
    gelu_value = 0.5 * pre_act * (1.0 + tangent)
    gelu_slope = 0.5 * (1.0 + tangent) + 0.5 * pre_act * (1.0 - tangent * tangent) * tanh_scale * (
        1.0 + 3.0 * cubic_term * pre_act * pre_act
    )
    return (gelu_value, gelu_slope)


def token_advantage(teacher_ids, adv_table):
    classes = adv_table.shape[0]
    class_hit = teacher_ids[:, None] == jnp.arange(classes, dtype=jnp.int32)[None, :]
    return jnp.sum(jnp.where(class_hit, adv_table[None, :], 0.0), axis=1)


def local_any(
    layer_input,
    gate_pre,
    up_pre,
    hidden_cot,
    teacher_ids,
    adv_table,
    gate_weight,
    up_weight,
    row_moments,
    col_moments,
):
    data_size = lax.axis_size("dp")
    model_size = lax.axis_size("mp")
    block_rows = gate_weight.shape[0]
    block_cols = gate_weight.shape[1]
    token_count = layer_input.shape[0]
    advantage = token_advantage(teacher_ids, adv_table)
    weighted = hidden_cot.astype(f32) * advantage[:, None]
    gelu_value, gelu_slope = gelu_pair(gate_pre.astype(f32))
    gate_grad = (weighted * up_pre.astype(f32) * gelu_slope).astype(bf16)
    up_grad = (weighted * gelu_value).astype(bf16)
    contract_last = (((1,), (1,)), ((), ()))
    contract_first = (((0,), (0,)), ((), ()))
    pieces = lax.all_gather((gate_weight, up_weight), "dp", axis=0, tiled=True)
    partial_sum = lax.dot_general(
        gate_grad, pieces[0], contract_last, preferred_element_type=f32
    ) + lax.dot_general(up_grad, pieces[1], contract_last, preferred_element_type=f32)
    input_grad = lax.psum_scatter(
        partial_sum.astype(bf16), "mp", scatter_dimension=1, tiled=True
    )
    grad_scale = 1.0 / math.sqrt(token_count * data_size)
    gate_term = lax.dot_general(layer_input, gate_grad, contract_first, preferred_element_type=f32)
    up_term = lax.dot_general(layer_input, up_grad, contract_first, preferred_element_type=f32)
    summed = lax.psum_scatter(
        jnp.concatenate([gate_term, up_term], axis=1).astype(bf16),
        "dp",
        scatter_dimension=0,
        tiled=True,
    ).astype(f32)
    grad_gate = summed[:, :block_cols] * grad_scale
    grad_up = summed[:, block_cols:] * grad_scale
    squares_gate = grad_gate * grad_gate
    squares_up = grad_up * grad_up
    row_local = jnp.stack([jnp.sum(squares_gate, axis=1), jnp.sum(squares_up, axis=1)])
    col_local = jnp.stack([jnp.sum(squares_gate, axis=0), jnp.sum(squares_up, axis=0)])
    row_total = lax.psum(row_local, "mp")
    col_total = lax.psum(col_local, "dp")
    new_rows = decay_rate * row_moments + (1.0 - decay_rate) * (
        row_total / (block_cols * model_size)
    )
    new_cols = decay_rate * col_moments + (1.0 - decay_rate) * (
        col_total / (block_rows * data_size)
    )
    scaled_gate = grad_gate / jnp.sqrt(new_rows[0][:, None] * new_cols[0][None, :])
    scaled_up = grad_up / jnp.sqrt(new_rows[1][:, None] * new_cols[1][None, :])
    square_sums = lax.psum(
        jnp.stack([jnp.sum(scaled_gate * scaled_gate), jnp.sum(scaled_up * scaled_up)]),
        ("dp", "mp"),
    )
    entry_count = block_rows * data_size * block_cols * model_size
    mean_square = square_sums / entry_count
    gate_update = scaled_gate / jnp.sqrt(mean_square[0] + 1e-06)
    up_update = scaled_up / jnp.sqrt(mean_square[1] + 1e-06)
    return (input_grad, gate_update, up_update, new_rows, new_cols)


def device_number(place):
    number = 0
    for coordinate, size in zip(place, GRID):
        number = number * size + coordinate
    return number


def pairs(target):
    out = []
    for z in range(GRID[0]):
        for x in range(GRID[1]):
            for y in range(GRID[2]):
                for c in range(GRID[3]):
                    place = target(z, x, y, c)
                    if place is not None:
                        out.append((device_number((z, x, y, c)), device_number(place)))
    return out


def flip_z(k):
    return pairs(lambda z, x, y, c: (z ^ k, x, y, c))


FLIP_X = pairs(lambda z, x, y, c: (z, 1 - x, y, c))
FLIP_Y = pairs(lambda z, x, y, c: (z, x, 1 - y, c))
FLIP_C = pairs(lambda z, x, y, c: (z, x, y, 1 - c))
MIDDLE = pairs(lambda z, x, y, c: (3 - z, x, y, c) if z in (1, 2) else None)
OUTWARD = pairs(lambda z, x, y, c: ({1: 0, 2: 3}[z], x, y, c) if z in (1, 2) else None)
INWARD = pairs(lambda z, x, y, c: ({0: 1, 3: 2}[z], x, y, c) if z in (0, 3) else None)


def home(first, half):
    return pairs(lambda z, x, y, c: (z ^ (first + c), x, z >> 1, z & 1) if y == half else None)


def home_from(core, k, half):
    return pairs(
        lambda z, x, y, c: (z ^ k, x, z >> 1, z & 1) if (y, c) == (half, core) else None
    )


def to_core(core):
    return pairs(lambda z, x, y, c: (z, x, y, core) if c != core else None)


def flip_y_of(core):
    return pairs(lambda z, x, y, c: (z, x, 1 - y, c) if c == core else None)


def send(value, permutation):
    return lax.ppermute(value, AXES, permutation)


def tie(*values):
    return lax.optimization_barrier(values)


def advantage_of(ids_ref, table_ref):
    ids = ids_ref[...]
    hit = ids == lax.broadcasted_iota(jnp.int32, (ids.shape[0], table_ref.shape[1]), 1)
    return jnp.sum(jnp.where(hit, table_ref[...], 0.0), axis=1, keepdims=True)


def gate_kernel(ids_ref, table_ref, cot_ref, gate_ref, up_ref, out_ref):
    weighted = cot_ref[...].astype(f32) * advantage_of(ids_ref, table_ref)
    slope = gelu_pair(gate_ref[...].astype(f32))[1]
    out_ref[...] = (weighted * up_ref[...].astype(f32) * slope).astype(bf16)


def up_kernel(ids_ref, table_ref, cot_ref, gate_ref, out_ref):
    weighted = cot_ref[...].astype(f32) * advantage_of(ids_ref, table_ref)
    out_ref[...] = (weighted * gelu_pair(gate_ref[...].astype(f32))[0]).astype(bf16)


def front(kernel, teacher_ids, adv_table, arrays):
    tokens, cols = arrays[0].shape
    rows = 128
    block = pl.BlockSpec((rows, cols), lambda i: (i, 0))
    return pl.pallas_call(
        kernel,
        grid=(tokens // rows,),
        in_specs=[
            pl.BlockSpec((rows, 1), lambda i: (i, 0)),
            pl.BlockSpec((1, adv_table.shape[0]), lambda i: (0, 0)),
        ]
        + [block] * len(arrays),
        out_specs=block,
        out_shape=jax.ShapeDtypeStruct((tokens, cols), bf16),
        cost_estimate=pl.CostEstimate(
            flops=tokens * cols, bytes_accessed=tokens * cols, transcendentals=0
        ),
    )(teacher_ids[:, None], adv_table[None, :], *arrays)


def dot_first(a, b):
    return lax.dot_general(a, b, (((0,), (0,)), ((), ())), preferred_element_type=f32)


def dot_last(a, b):
    return lax.dot_general(a, b, (((1,), (1,)), ((), ())), preferred_element_type=f32)


def sum_over(value, permutations):
    for permutation in permutations:
        value = value + send(value, permutation)
    return value


OVER_DP = (FLIP_X, flip_z(1), flip_z(2))
OVER_MP = (FLIP_C, FLIP_Y)


def local_block(
    layer_input,
    gate_pre,
    up_pre,
    hidden_cot,
    teacher_ids,
    adv_table,
    gate_weight,
    up_weight,
    row_moments,
    col_moments,
):
    data_size = lax.axis_size("dp")
    model_size = lax.axis_size("mp")
    rows, cols = gate_weight.shape
    tokens = layer_input.shape[0]
    dp = lax.axis_index("dp")
    m = lax.axis_index("mp")
    z, x = dp // 2, dp % 2
    y, c = m // 2, m % 2
    piece_rows = tokens // model_size
    plane = 2 * rows
    edge = cols * 4 // 10 // 128 * 128
    up_spans = [slice(0, edge), slice(edge, cols)]
    grad_scale = 1.0 / math.sqrt(tokens * data_size)

    def plane_rows(own, other):
        both = jnp.zeros((plane, cols), bf16)
        both = lax.dynamic_update_slice(both, own, (x * rows, 0))
        return lax.dynamic_update_slice(both, other, ((1 - x) * rows, 0))

    def over_core(first, second):
        keep = jnp.where(c == 0, first, second)
        away = jnp.where(c == 0, second, first).astype(bf16)
        return keep, away

    def over_y(block):
        part = tokens // 2
        keep = lax.dynamic_slice(block, (y * part, 0), (part, plane))
        away = lax.dynamic_slice(block, ((1 - y) * part, 0), (part, plane)).astype(bf16)
        return keep, away

    def gradient(keep, recv):
        return (keep + recv.astype(f32)) * grad_scale

    mine = lax.dynamic_slice(layer_input, (m * piece_rows, 0), (piece_rows, layer_input.shape[1]))
    piece = [
        send(lax.dynamic_slice(mine, (0, (z ^ k) * plane), (piece_rows, plane)), flip_z(k))
        for k in (1, 2, 3)
    ]
    g = front(gate_kernel, teacher_ids, adv_table, (hidden_cot, gate_pre, up_pre))
    u = front(up_kernel, teacher_ids, adv_table, (hidden_cot, gate_pre))
    piece, g, u, gate_weight, up_weight = tie(piece, g, u, gate_weight, up_weight)
    gate_other = send(gate_weight, FLIP_X)

    g_near = send(g, flip_z(1))
    g_over = send(g, MIDDLE)
    u_near = send(u, flip_z(1))
    u_over = send(u, MIDDLE)
    piece = jnp.stack(piece)
    g_near, g_over, gate_other, piece, up_weight = tie(g_near, g_over, gate_other, piece, up_weight)
    up_other = send(up_weight, FLIP_X)

    g_far = send(g_over, OUTWARD)
    g_near_over = send(g_near, MIDDLE)
    piece_y = send(piece, FLIP_Y)
    gate_rows = plane_rows(gate_weight, gate_other)
    u_near, u_over, gate_rows, up_other, piece, piece_y = tie(
        u_near, u_over, gate_rows, up_other, piece, piece_y
    )
    up_rows = plane_rows(up_weight, up_other)

    u_near_over = send(u_near, MIDDLE)
    pieces = jnp.stack([piece, piece_y])
    pieces_c = send(pieces, FLIP_C)
    early = dot_last(jnp.concatenate([g, g_near], axis=0), gate_rows)
    early = early + dot_last(jnp.concatenate([u, u_near], axis=0), up_rows)
    early_keep, early_away = over_core(early[:tokens], early[tokens:])
    early_recv = send(early_away, FLIP_C)
    g_far, g_near_over, pieces, pieces_c, early_keep, early_recv, u_over = tie(
        g_far, g_near_over, pieces, pieces_c, early_keep, early_recv, u_over
    )

    g_farthest = send(g_near_over, OUTWARD)
    u_far = send(u_over, OUTWARD)
    far = jnp.zeros((3, model_size, piece_rows, plane), bf16)
    for part, place in ((pieces[0], m), (pieces_c[0], m ^ 1), (pieces[1], m ^ 2), (pieces_c[1], m ^ 3)):
        far = lax.dynamic_update_slice(far, part[:, None], (0, place, 0, 0))
    own_inputs = lax.dynamic_slice(layer_input, (0, z * plane), (tokens, plane))
    inputs = jnp.concatenate([own_inputs, far.reshape(3 * tokens, plane)])
    near_tokens = 3 * tokens
    inputs_keep = lax.dynamic_slice(inputs, (0, x * rows), (4 * tokens, rows))
    inputs_away = lax.dynamic_slice(inputs, (0, (1 - x) * rows), (4 * tokens, rows))

    inputs, early_keep, early_recv = tie(inputs, early_keep, early_recv)
    early_keep, early_away = over_y(early_keep + early_recv.astype(f32))
    early_recv = send(early_away, FLIP_Y)

    def near_products(block):
        return dot_first(inputs_away[:near_tokens], block), dot_first(inputs_keep[:near_tokens], block)

    def last_products(block, near, span):
        away, keep = near
        away = away[:, span] + dot_first(inputs_away[near_tokens:], block)
        return away.astype(bf16), keep[:, span] + dot_first(inputs_keep[near_tokens:], block)

    g_third = g_near_over + g_far
    g_products = near_products(jnp.concatenate([g, g_near, g_third], axis=0))
    early_sum = (early_keep + early_recv.astype(f32)).astype(bf16)
    u_near_over, g_farthest, g_products, inputs_keep, inputs_away, early_sum = tie(
        u_near_over, g_farthest, g_products, inputs_keep, inputs_away, early_sum
    )

    u_farthest = [send(u_near_over[:, up_spans[0]], OUTWARD)]
    g_last = g_over + g_farthest
    away, g_keep = last_products(g_last, g_products, slice(None))
    g_recv = send(away, FLIP_X)
    early_home = [send(early_sum, home(0, h)) for h in range(2)]
    u_far, early_home, g_keep, g_last, u_near_over = tie(u_far, early_home, g_keep, g_last, u_near_over)

    u_farthest.append(send(u_near_over[:, up_spans[1]], OUTWARD))
    u_third = u_near_over + u_far
    u_products = near_products(jnp.concatenate([u, u_near, u_third], axis=0))
    third = dot_last(g_third, gate_rows) + dot_last(u_third, up_rows)
    third_recv = send(third.astype(bf16), to_core(0))
    u_products, third, third_recv, u_farthest[0], g_recv = tie(
        u_products, third, third_recv, u_farthest[0], g_recv
    )

    block = u_over[:, up_spans[0]] + u_farthest[0]
    away, first_keep = last_products(block, u_products, up_spans[0])
    first_recv = send(away, FLIP_X)
    last = dot_last(g_last, gate_rows) + dot_last(block, up_rows[:, up_spans[0]])
    third_keep, third_away = over_y(third + third_recv.astype(f32))
    third_recv = send(third_away, flip_y_of(0))
    last, first_keep, first_recv, u_farthest[1], third_keep, third_recv = tie(
        last, first_keep, first_recv, u_farthest[1], third_keep, third_recv
    )

    block = u_over[:, up_spans[1]] + u_farthest[1]
    away, second_keep = last_products(block, u_products, up_spans[1])
    second_recv = send(away, FLIP_X)
    last = last + dot_last(block, up_rows[:, up_spans[1]])
    late_recv = send(last.astype(bf16), to_core(1))
    third_sum = (third_keep + third_recv.astype(f32)).astype(bf16)
    third_home = [send(third_sum, home_from(0, 2, h)) for h in range(2)]
    late_keep, late_away = over_y(last + late_recv.astype(f32))
    gate_gradient = gradient(g_keep, g_recv)
    gate_row = jnp.sum(gate_gradient * gate_gradient, axis=1)
    gate_col = jnp.sum(gate_gradient * gate_gradient, axis=0)
    late_away, late_keep, gate_row, gate_col, gate_gradient, second_keep = tie(
        late_away, late_keep, gate_row, gate_col, gate_gradient, second_keep
    )
    late_recv = send(late_away, flip_y_of(1))
    late_recv, second_recv, third_home = tie(late_recv, second_recv, third_home)
    late_sum = (late_keep + late_recv.astype(f32)).astype(bf16)
    late_home = [send(late_sum, home_from(1, 3, h)) for h in range(2)]

    entry_count = rows * data_size * cols * model_size
    up_gradient = jnp.concatenate(
        [gradient(first_keep, first_recv), gradient(second_keep, second_recv)], axis=1
    )
    gradients = (gate_gradient, up_gradient)
    squares = up_gradient * up_gradient
    row_total = sum_over(jnp.stack([gate_row, jnp.sum(squares, axis=1)]), OVER_MP)
    new_rows = decay_rate * row_moments + (1.0 - decay_rate) * (row_total / (cols * model_size))
    inverse = 1.0 / new_rows
    column_sums = jnp.concatenate(
        [gate_col, jnp.sum(squares, axis=0)]
        + [jnp.sum(v * v * inverse[k][:, None], axis=0) for k, v in enumerate(gradients)]
    )
    column_sums = sum_over(column_sums, OVER_DP).reshape(2, 2, cols)
    new_cols = decay_rate * col_moments + (1.0 - decay_rate) * (
        column_sums[0] / (rows * data_size)
    )
    square_sums = jnp.sum(column_sums[1] / new_cols, axis=1)
    square_sums = sum_over(jnp.broadcast_to(square_sums[:, None], (2, 128)), OVER_MP)[:, :1]
    row_factor = lax.rsqrt(new_rows) * lax.rsqrt(square_sums / entry_count + 1e-06)
    col_factor = lax.rsqrt(new_cols)
    updates = [
        v * row_factor[k][:, None] * col_factor[k][None, :] for k, v in enumerate(gradients)
    ]
    input_grad = jnp.concatenate(
        [early_home[h] + third_home[h] + late_home[h] for h in range(2)], axis=0
    )
    return input_grad, updates[0], updates[1], new_rows, new_cols


def solution(mesh):
    in_specs = (
        P("dp", None),
        P("dp", "mp"),
        P("dp", "mp"),
        P("dp", "mp"),
        P("dp"),
        P(),
        P("dp", "mp"),
        P("dp", "mp"),
        P(None, "dp"),
        P(None, "mp"),
    )
    out_specs = (P("dp", "mp"), P("dp", "mp"), P("dp", "mp"), P(None, "dp"), P(None, "mp"))
    fits = (mesh.shape["dp"], mesh.shape["mp"]) == (GRID[0] * GRID[1], GRID[2] * GRID[3])
    local = local_block if fits else local_any
    return jax.shard_map(local, mesh=mesh, in_specs=in_specs, out_specs=out_specs, check_vma=False)
```
